128 devices in a mesh: col: 4 (over z), sec: 32 (over y, x, core).
Axes of the slice: x: 4, y: 4, z: 4, core: 2. Of those that a mesh axis runs over, the one named last changes fastest.
Arguments:
- site_tensor: float32 [512, 32, 1536], P('col', 'sec')
- left_env: float32 [32, 5, 512, 512], P('sec'), as said below
- right_env: float32 [32, 5, 512, 512], P('sec', None, None, 'col'), as said below
- bond_env: float32 [32, 5, 512, 512], P('sec'), as said below
- sector_sizes: int32 [32], P('sec'), may hold values from 1 to 512, as said below
Outputs:
- evolved_site: float32 [512, 32, 1536], P('col', 'sec')
- evolved_bond: float32 [512, 32, 512], P('col', 'sec')
The draws below stay inside these ranges and needn't reach their ends.
Inputs may be any that keep to these rules, and one draw needn't show every extreme that they name: `sector_sizes`: the sizes sum to 8192. Every tensor and environment block is zero outside the live states of its sectors. For a in 0, 1, 4 the blocks left_env[t, a] are symmetric, and left_env[t, 3] is the transpose of left_env[t - 1, 2] (zero for t = 0). `right_env`: same structure as left_env. `bond_env`: same structure as left_env.
All inputs are finite; a program needn't handle non-finite values.
Results may differ from the reference program's by a relative error of at most 0.0003.
Values sent between devices are 32-bit elements; how exact they have to be, the bound alone decides.
No kernel may reach another device: no remote copies, remote signals or barrier semaphores. Data moves between devices by JAX's collectives and lax.ppermute only.
A program may use at most 192 MiB of HBM per device.

```python
import math
import jax
import jax.numpy as jnp
from jax import lax

M = 512
KRYLOV = 4
NSEC = 32


def sector_draw(key):
    base_key = jax.random.fold_in(key, 101)
    first_key, second_key = jax.random.split(base_key)
    half_block = M // 2
    offsets = jax.random.randint(first_key, (NSEC,), 0, half_block)
    offsets = offsets.at[0].set(half_block - 1).at[1].set(0)
    offsets = offsets.at[2].set(jnp.minimum(offsets[2], half_block - 2))
    counts = half_block + offsets - jnp.roll(offsets, -1)
    counts = counts.at[0].add(1).at[1].add(-1)
    rotation = jax.random.randint(second_key, (), 0, NSEC)
    return counts[(jnp.arange(NSEC) + rotation) % NSEC].astype(jnp.int32)


def live_of(key):
    counts = sector_draw(key)
    return (jnp.arange(M)[None, :] < counts[:, None]).astype(jnp.float32)


def neighbour(mask, offset):
    return jnp.pad(mask, ((1, 1), (0, 0)))[1 + offset:1 + offset + NSEC]


def environment(key, salt):
    live = live_of(key)
    draw_key = jax.random.fold_in(key, salt)
    first_key = jax.random.fold_in(draw_key, 0)
    position = jnp.arange(NSEC, dtype=jnp.float32) / max(NSEC - 1, 1)
    gaussian = jax.random.normal(first_key, (NSEC, 5, M, M), jnp.float32)
    diagonal_height = 1.0 + 1.2 * position
    gaussian = gaussian / math.sqrt(M)
    rows_live = live
    paired = rows_live[:, :, None] * rows_live[:, None, :]
    diagonal_block = (live * diagonal_height[:, None])[:, :, None] * jnp.eye(M, dtype=jnp.float32)[None]

    def symmetric(index):
        return (gaussian[:, index] + jnp.swapaxes(gaussian[:, index], 1, 2)) * (paired / math.sqrt(2.0))
    raising = gaussian[:, 2] * rows_live[:, :, None] * neighbour(rows_live, 1)[:, None, :]
    lowering = jnp.swapaxes(jnp.pad(raising, ((1, 0), (0, 0), (0, 0)))[:NSEC], 1, 2)
    return jnp.stack([symmetric(0) + diagonal_block, symmetric(1), raising, lowering, symmetric(4) + diagonal_block], axis=1)


def draw_left_env(key, part):
    return environment(key, 201)


def draw_right_env(key, part):
    return environment(key, 202)


def draw_bond_env(key, part):
    return environment(key, 203)


def draw_site_tensor(key, part):
    live = live_of(key)
    draw_key = jax.random.fold_in(key, 204)
    row_position = jnp.arange(M, dtype=jnp.float32) / M
    values = jax.random.normal(draw_key, (M, NSEC, 3, M), jnp.float32)
    row_rise = 1.0 + 0.8 * row_position
    left_live = jnp.stack([neighbour(live, -1), live, neighbour(live, 1)], axis=1)
    values = values * jnp.transpose(live)[:, :, None, None] * left_live[None] * row_rise[:, None, None, None]
    return values.reshape(M, NSEC, 3 * M)


def draw_sector_sizes(key, part):
    return sector_draw(key)


def setup_inputs(seed: int = 0) -> dict:
    splits = jax.random.split(jax.random.key(seed), 6)
    return {
        "site_tensor": draw_site_tensor(jax.random.fold_in(splits[5], 71), 0),
        "left_env": draw_left_env(jax.random.fold_in(splits[5], 71), 0),
        "right_env": draw_right_env(jax.random.fold_in(splits[5], 71), 0),
        "bond_env": draw_bond_env(jax.random.fold_in(splits[5], 71), 0),
        "sector_sizes": draw_sector_sizes(jax.random.fold_in(splits[5], 71), 0),
    }


HIGH_PREC = lax.Precision.HIGHEST
SECTOR_SHIFT = (0, 0, 1, -1, 0)
ROOT_TWO = math.sqrt(2.0)
ANISOTROPY = 0.5
TIME_STEP = 0.1
ONE_SITE_TERMS = ((0, 0, 0, 0, 1.0), (0, 0, 1, 1, 1.0), (0, 0, 2, 2, 1.0), (1, 0, 0, 0, 1.0), (1, 0, 2, 2, -1.0), (2, 0, 0, 1, ROOT_TWO), (2, 0, 1, 2, ROOT_TWO), (3, 0, 1, 0, ROOT_TWO), (3, 0, 2, 1, ROOT_TWO), (4, 0, 0, 0, ANISOTROPY), (4, 0, 2, 2, ANISOTROPY), (4, 1, 0, 0, 1.0), (4, 1, 2, 2, -1.0), (4, 2, 1, 0, ROOT_TWO / 2), (4, 2, 2, 1, ROOT_TWO / 2), (4, 3, 0, 1, ROOT_TWO / 2), (4, 3, 1, 2, ROOT_TWO / 2), (4, 4, 0, 0, 1.0), (4, 4, 1, 1, 1.0), (4, 4, 2, 2, 1.0))
ZERO_SITE_TERMS = ((0, 0, 0, 0, 1.0), (1, 1, 0, 0, 1.0), (2, 2, 0, 0, 1.0), (3, 3, 0, 0, 1.0), (4, 4, 0, 0, 1.0))

def small_exp(matrix):
    dimension = matrix.shape[0]
    identity = jnp.eye(dimension, dtype=jnp.float32)
    scaled = matrix / 16.0
    result = identity
    for degree in range(8, 0, -1):
        result = identity + jnp.dot(scaled, result, precision=HIGH_PREC) / degree
    for squaring in range(4):
        result = jnp.dot(result, result, precision=HIGH_PREC)
    return result

def tridiagonal(alpha_list, beta_list):
    diagonal_part = jnp.diag(jnp.stack(alpha_list))
    upper_part = jnp.diag(jnp.stack(beta_list), 1)
    return diagonal_part + upper_part + upper_part.T

def apply_left(fetch_block, left_of, term_list, spin_count, wanted):
    columns = []
    for spin_out in range(spin_count):
        summed = None
        for a, b, spin_row, spin_in, factor in term_list:
            if spin_row == spin_out and b in wanted:
                product = factor * jnp.einsum('rtk,tlk->rtl', fetch_block(b, spin_in), left_of(a, spin_out), precision=HIGH_PREC)
                summed = product if summed is None else summed + product
        if summed is None:
            summed = jnp.zeros_like(fetch_block(0, spin_out))
        columns.append(summed)
    return jnp.concatenate(columns, axis=2)

def apply_ham(vector, spin_count, left_of, term_list, right_env):
    sector_count = vector.shape[1]
    block_size = vector.shape[2] // spin_count
    widened = jnp.pad(vector, ((0, 0), (1, 1), (0, 0)))

    def source(which_b, spin_in):
        lowest = 1 + SECTOR_SHIFT[which_b]
        return widened[:, lowest:lowest + sector_count, spin_in * block_size:(spin_in + 1) * block_size]
    summed = jnp.zeros_like(vector)
    for b in range(5):
        mixed = apply_left(source, left_of, term_list, spin_count, (b,))
        summed = summed + jnp.einsum('trc,ctx->rtx', right_env[:, b], mixed, precision=HIGH_PREC)
    return summed

def evolve(start, apply_fn, sign):
    norm_zero = jnp.sqrt(jnp.sum(start * start))
    krylov_basis = [start / norm_zero]
    alpha_list = []
    beta_list = []
    for krylov_step in range(KRYLOV):
        image = apply_fn(krylov_basis[krylov_step])
        if krylov_step > 0:
            image = image - beta_list[krylov_step - 1] * krylov_basis[krylov_step - 1]
        alpha_now = jnp.sum(krylov_basis[krylov_step] * image)
        alpha_list.append(alpha_now)
        if krylov_step + 1 < KRYLOV:
            image = image - alpha_now * krylov_basis[krylov_step]
            beta_now = jnp.sqrt(jnp.sum(image * image))
            beta_list.append(beta_now)
            krylov_basis.append(image / beta_now)
    weights = small_exp(sign * TIME_STEP * tridiagonal(alpha_list, beta_list))[:, 0]
    result = weights[0] * krylov_basis[0]
    for krylov_step in range(1, KRYLOV):
        result = result + weights[krylov_step] * krylov_basis[krylov_step]
    return norm_zero * result

def reference(site_tensor, left_env, right_env, bond_env, sector_sizes):
    sector_count = site_tensor.shape[1]
    block_size = left_env.shape[2]
    left_wide = jnp.pad(left_env, ((1, 1), (0, 0), (0, 0), (0, 0)))

    def site_left(a, spin_out):
        return left_wide[spin_out:spin_out + sector_count, a]

    def bond_left(a, spin_out):
        return bond_env[:, a]
    evolved_site = evolve(site_tensor, lambda vector: apply_ham(vector, 3, site_left, ONE_SITE_TERMS, right_env), -1.0)
    gram_matrix = jnp.einsum('rtx,stx->trs', evolved_site, evolved_site, precision=HIGH_PREC)
    live_mask = (jnp.arange(block_size)[None, :] < sector_sizes[:, None]).astype(jnp.float32)
    gram_matrix = gram_matrix + (1.0 - live_mask)[:, :, None] * jnp.eye(block_size, dtype=jnp.float32)[None]
    factor_lower = jnp.linalg.cholesky(gram_matrix)
    masked = factor_lower * live_mask[:, :, None] * live_mask[:, None, :]
    bond_start = jnp.transpose(masked, (1, 0, 2)) / math.sqrt(3.0 * block_size)
    evolved_bond = evolve(bond_start, lambda vector: apply_ham(vector, 1, bond_left, ZERO_SITE_TERMS, right_env), 1.0)
    return (evolved_site, evolved_bond)
```

```python
import math

import jax
import jax.numpy as jnp
from jax import lax
from jax.sharding import PartitionSpec as P

KRYLOV = 4
HIGHEST = lax.Precision.HIGHEST
HIGH = lax.Precision.HIGH
ROOT_TWO = math.sqrt(2.0)
ANISOTROPY = 0.5
TIME_STEP = 0.1


def small_exp(matrix):
    dimension = matrix.shape[0]
    identity = jnp.eye(dimension, dtype=jnp.float32)
    scaled = matrix / 16.0

    def mul(left, right):
        return jnp.sum(left[:, :, None] * right[None, :, :], axis=1)

    result = identity
    for degree in range(8, 0, -1):
        result = identity + mul(scaled, result) / degree
    for squaring in range(4):
        result = mul(result, result)
    return result


def tridiagonal(alpha_list, beta_list):
    diagonal_part = jnp.diag(jnp.stack(alpha_list))
    upper_part = jnp.diag(jnp.stack(beta_list), 1)
    return diagonal_part + upper_part + upper_part.T


def sector_perms(mesh_shape):
    ny, nx, nc = mesh_shape

    def perm(move):
        pairs = []
        for y in range(ny):
            for x in range(nx):
                for k in range(nc):
                    y2, x2, k2 = move(y, x, k)
                    source = (y * nx + x) * nc + k
                    target = ((y2 % ny) * nx + x2 % nx) * nc + k2 % nc
                    pairs.append((source, target))
        return pairs

    stages = [[perm(lambda y, x, k: (y, x, k + 1))]]
    stages.append([perm(lambda y, x, k, d=d: (y, x + d, k)) for d in range(1, nx)])
    stages.append([perm(lambda y, x, k, d=d: (y + d, x, k)) for d in range(1, ny)])
    return stages


STAGES = sector_perms((4, 4, 2))


def sum_over_sectors(values):
    packed = jnp.stack(values)
    for stage in STAGES:
        received = [lax.ppermute(packed, "sec", pairs) for pairs in stage]
        for part in received:
            packed = packed + part
    return [packed[i] for i in range(len(values))]


def to_next(block):
    count = lax.axis_size("sec")
    return lax.ppermute(block, "sec", [(i, i + 1) for i in range(count - 1)])


def to_previous(block):
    count = lax.axis_size("sec")
    return lax.ppermute(block, "sec", [(i + 1, i) for i in range(count - 1)])


def gather_col(block, axis):
    return lax.all_gather(block, "col", axis=axis, tiled=True)


def mm(left, right):
    return jnp.dot(left, right, precision=HIGH)


def evolve(start, apply_fn, sign, scale_of):
    raw = apply_fn(start)
    norm_zero = scale_of()
    inverse = 1.0 / norm_zero
    u_list = [start * inverse]
    y_list = [raw * inverse]
    gammas = [jnp.float32(1.0)]
    alphas = []
    betas = []
    for step in range(KRYLOV):
        u_now, y_now = u_list[-1], y_list[-1]
        partial = [jnp.sum(u_now * u_now), jnp.sum(u_now * y_now)]
        ahead = apply_fn(y_now) if step + 1 < KRYLOV else None
        norm_sq, cross = sum_over_sectors(partial)
        if step > 0:
            beta = jnp.sqrt(norm_sq)
            betas.append(beta)
            gammas.append(1.0 / beta)
            alphas.append(cross / norm_sq)
        else:
            alphas.append(cross)
        if step + 1 < KRYLOV:
            gamma = gammas[-1]
            u_next = gamma * (y_now - alphas[-1] * u_now)
            y_next = gamma * (ahead - alphas[-1] * y_now)
            if step > 0:
                back = betas[-1] * gammas[-2]
                u_next = u_next - back * u_list[-2]
                y_next = y_next - back * y_list[-2]
            u_list.append(u_next)
            y_list.append(y_next)
    weights = small_exp(sign * TIME_STEP * tridiagonal(alphas, betas))[:, 0]
    result = (norm_zero * weights[0]) * u_list[0]
    for step in range(1, KRYLOV):
        result = result + (norm_zero * weights[step] * gammas[step]) * u_list[step]
    return result


def body(site_tensor, left_env, right_env, bond_env, sector_sizes):
    col_rows = site_tensor.shape[0]
    block_size = left_env.shape[2]
    size = block_size
    sector = lax.axis_index("sec")
    last = lax.axis_size("sec") - 1

    left = left_env[0]
    site_full = gather_col(site_tensor[:, 0], 0)
    right = gather_col(right_env[0], 2)

    send_up = jnp.stack([left[0] + left[1] + ANISOTROPY * left[4], left[4]])
    send_down = jnp.stack([left[0] - left[1] + ANISOTROPY * left[4], left[4]])
    below = to_next(send_up)
    above = to_previous(send_down)
    raise_here = jnp.where(sector < last, ROOT_TWO * left[2], 0.0)
    lower_here = jnp.where(sector > 0, ROOT_TWO * left[3], 0.0)
    right_plus = right[4] + right[1]
    right_minus = right[4] - right[1]
    half = ROOT_TWO / 2
    up_matrix = half * right[2].T
    down_matrix = half * right[3].T

    def apply_site(vector):
        x0, x1, x2 = (vector[:, s * size : (s + 1) * size] for s in range(3))
        z1 = mm(x1, left[4])
        z0 = mm(x0, below[1])
        z2 = mm(x2, above[1])
        from_above = to_previous(mm(down_matrix, jnp.concatenate([z0, z1], axis=1)))
        from_below = to_next(mm(up_matrix, jnp.concatenate([z1, z2], axis=1)))
        p0 = mm(x0, below[0]) + mm(x1, lower_here)
        p1 = mm(x1, left[0]) + mm(x0, lower_here.T) + mm(x2, raise_here.T)
        p2 = mm(x2, above[0]) + mm(x1, raise_here)
        y0 = mm(right[0], p0) + mm(right_plus, z0)
        y1 = mm(right[0], p1) + mm(right[4], z1)
        y2 = mm(right[0], p2) + mm(right_minus, z2)
        y0 = y0 + from_below[:, :size]
        y1 = y1 + from_below[:, size:] + from_above[:, :size]
        y2 = y2 + from_above[:, size:]
        return jnp.concatenate([y0, y1, y2], axis=1)

    def site_norm():
        (norm_sq,) = sum_over_sectors([jnp.sum(site_full * site_full)])
        return jnp.sqrt(norm_sq)

    evolved = evolve(site_full, apply_site, -1.0, site_norm)
    gram = lax.dot_general(evolved, evolved, (((1,), (1,)), ((), ())), precision=HIGHEST)
    live = (jnp.arange(size) < sector_sizes[0]).astype(jnp.float32)
    gram = gram + (1.0 - live)[:, None] * jnp.eye(size, dtype=jnp.float32)
    factor = jnp.linalg.cholesky(gram[None])[0]
    start = factor * live[:, None] * live[None, :] / math.sqrt(3.0 * block_size)

    bond = bond_env[0]
    down_bond = ROOT_TWO * bond[3]
    up_bond = ROOT_TWO * bond[2]

    def apply_bond(vector):
        from_above = to_previous(mm(down_matrix, mm(vector, down_bond)))
        from_below = to_next(mm(up_matrix, mm(vector, up_bond)))
        y = mm(right[0], mm(vector, bond[0]))
        y = y + mm(right[1], mm(vector, bond[1]))
        y = y + mm(right[4], mm(vector, bond[4]))
        return y + from_above + from_below

    def bond_norm():
        (norm_sq,) = sum_over_sectors([jnp.sum(start * start)])
        return jnp.sqrt(norm_sq)

    evolved_bond = evolve(start, apply_bond, 1.0, bond_norm)

    offset = lax.axis_index("col") * col_rows
    out_site = lax.dynamic_slice_in_dim(evolved, offset, col_rows, 0)[:, None, :]
    out_bond = lax.dynamic_slice_in_dim(evolved_bond, offset, col_rows, 0)[:, None, :]
    return (out_site, out_bond)


def solution(mesh):
    in_specs = (
        P("col", "sec", None),
        P("sec", None, None, None),
        P("sec", None, None, "col"),
        P("sec", None, None, None),
        P("sec"),
    )
    out_specs = (P("col", "sec", None), P("col", "sec", None))
    return jax.shard_map(body, mesh=mesh, in_specs=in_specs, out_specs=out_specs, check_vma=False)
```

```python
import functools
import math

import jax
import jax.numpy as jnp
from jax import lax
from jax.experimental import pallas as pl
from jax.experimental.pallas import tpu as pltpu
from jax.sharding import PartitionSpec as P

KRYLOV = 4
HIGHEST = lax.Precision.HIGHEST
HIGH = lax.Precision.HIGH
ROOT_TWO = math.sqrt(2.0)
ANISOTROPY = 0.5
TIME_STEP = 0.1
VMEM_LIMIT = 48 * 1024 * 1024
ROWS = 16


def to_next(block):
    count = lax.axis_size("sec")
    return lax.ppermute(block, "sec", [(i, i + 1) for i in range(count - 1)])


def to_previous(block):
    count = lax.axis_size("sec")
    return lax.ppermute(block, "sec", [(i + 1, i) for i in range(count - 1)])


def gather_col(block, axis):
    return lax.all_gather(block, "col", axis=axis, tiled=True)


def mm(left, right):
    return jnp.dot(left, right, precision=HIGH)


def params():
    return pltpu.CompilerParams(vmem_limit_bytes=VMEM_LIMIT)


def exchange(rows, axis):
    count = lax.axis_size(axis) if isinstance(axis, str) else lax.axis_size(axis[0]) * lax.axis_size(axis[1])
    sent = jnp.broadcast_to(rows[None], (count,) + rows.shape)
    return lax.all_to_all(sent, axis, 0, 0)


def sum_over_col(rows):
    count = lax.axis_size("col")
    parts = [
        lax.ppermute(rows, "col", [(i, (i + step) % count) for i in range(count)])
        for step in range(1, count)
    ]
    for part in parts:
        rows = rows + part
    return rows


def dot_rows_kernel(a_ref, out_ref):
    a = a_ref[...]
    out_ref[...] = jnp.full(out_ref.shape, jnp.sum(a * a))


def norm_rows(block):
    return pl.pallas_call(
        dot_rows_kernel,
        out_shape=jax.ShapeDtypeStruct((8, 128), jnp.float32),
        compiler_params=params(),
    )(block)


def inverse_norm_kernel(parts_ref, out_ref):
    out_ref[...] = 1.0 / jnp.sqrt(jnp.sum(parts_ref[...], axis=0))


def inverse_norm(parts):
    return pl.pallas_call(
        inverse_norm_kernel,
        out_shape=jax.ShapeDtypeStruct((8, 128), jnp.float32),
        compiler_params=params(),
    )(parts)


def first_combine_kernel(spins, nloc, *refs):
    scale_ref, x_ref = refs[0], refs[1]
    part_refs = refs[2 : 2 + nloc]
    y_ref, sums_ref = refs[2 + nloc], refs[3 + nloc]
    nu = scale_ref[0:1, 0:1]
    size = y_ref.shape[2]
    cross = jnp.float32(0.0)
    square = jnp.float32(0.0)
    index = 0
    for s in range(spins):
        total = None
        for part in spin_parts(spins, s):
            value = part_refs[index][...]
            index += 1
            total = value if total is None else total + value
        y = total * nu
        y_ref[s] = y
        cross += jnp.sum(x_ref[:, s * size : (s + 1) * size] * nu * y)
        square += jnp.sum(y * y)

    @pl.when(pl.program_id(0) == 0)
    def _():
        sums_ref[...] = jnp.zeros_like(sums_ref)

    row = lax.broadcasted_iota(jnp.int32, sums_ref.shape, 0)
    sums_ref[...] += jnp.where(row == 0, cross, jnp.where(row == 1, square, 0.0))


def spin_parts(spins, s):
    if spins == 1:
        return range(3)
    return range((2, 3, 2)[s])


def first_combine(x, nu, parts, spins):
    size = x.shape[0]
    step = 128
    spec = pl.BlockSpec((step, size), lambda i: (i, 0))
    return pl.pallas_call(
        functools.partial(first_combine_kernel, spins, len(parts)),
        grid=(size // step,),
        in_specs=[
            pl.BlockSpec((8, 128), lambda i: (0, 0)),
            pl.BlockSpec((step, spins * size), lambda i: (i, 0)),
        ]
        + [spec] * len(parts),
        out_specs=[
            pl.BlockSpec((spins, step, size), lambda i: (0, i, 0)),
            pl.BlockSpec((8, 128), lambda i: (0, 0)),
        ],
        out_shape=[
            jax.ShapeDtypeStruct((spins, size, size), jnp.float32),
            jax.ShapeDtypeStruct((8, 128), jnp.float32),
        ],
        compiler_params=params(),
    )(nu, x, *parts)


def shift_kernel(nu_ref, parts_ref, out_ref):
    total = jnp.sum(parts_ref[...], axis=0)
    row = lax.broadcasted_iota(jnp.int32, out_ref.shape, 0)
    sigma = total[0:1]
    tau = 1.0 / jnp.sqrt(total[1:2])
    out_ref[...] = jnp.where(row == 0, sigma, jnp.where(row == 1, tau, nu_ref[...]))


def shift_rows(nu, parts):
    return pl.pallas_call(
        shift_kernel,
        out_shape=jax.ShapeDtypeStruct((8, 128), jnp.float32),
        compiler_params=params(),
    )(nu, parts)


def combine_kernel(second, spins, count, *refs):
    scale_ref = refs[0]
    sigma, tau, nu = scale_ref[0:1, 0:1], scale_ref[1:2, 0:1], scale_ref[2:3, 0:1]
    w_ref = refs[1]
    x_ref = refs[2] if second else None
    base = 3 if second else 2
    part_refs = refs[base : base + count]
    out_ref = refs[base + count]
    size = out_ref.shape[2]
    index = 0
    for s in range(spins):
        total = None
        for part in spin_parts(spins, s):
            value = part_refs[index][...]
            index += 1
            total = value if total is None else total + value
        if second:
            x = x_ref[:, s * size : (s + 1) * size]
            inner = w_ref[s] - sigma * (nu * x)
            out_ref[s] = tau * tau * ((total - sigma * w_ref[s]) - sigma * inner)
        else:
            out_ref[s] = tau * (total - sigma * w_ref[s])


def combine(scales, w, x, parts, spins):
    size = w.shape[1]
    step = 128
    spec = pl.BlockSpec((step, size), lambda i: (i, 0))
    state = pl.BlockSpec((spins, step, size), lambda i: (0, i, 0))
    second = x is not None
    arrays = [scales, w] + ([x] if second else []) + list(parts)
    specs = [pl.BlockSpec((8, 128), lambda i: (0, 0)), state]
    if second:
        specs.append(pl.BlockSpec((step, spins * size), lambda i: (i, 0)))
    return pl.pallas_call(
        functools.partial(combine_kernel, second, spins, len(parts)),
        grid=(size // step,),
        in_specs=specs + [spec] * len(parts),
        out_specs=state,
        out_shape=jax.ShapeDtypeStruct((spins, size, size), jnp.float32),
        compiler_params=params(),
    )(*arrays)


PAIRS = [(i, j) for j in range(5) for i in range(j + 1) if (i, j) != (4, 4)]


def gram_kernel(spins, count, *refs):
    scale_ref, x_ref, y_ref, w2_ref, w3_ref = refs[:5]
    part_refs = refs[5 : 5 + count]
    out_ref = refs[5 + count]
    sigma, tau, nu = scale_ref[0:1, 0:1], scale_ref[1:2, 0:1], scale_ref[2:3, 0:1]
    sums = [jnp.zeros((1, 128), jnp.float32)] * len(PAIRS)
    index = 0
    for s in range(spins):
        total = None
        for part in spin_parts(spins, s):
            value = part_refs[index][...]
            index += 1
            total = value if total is None else total + value
        w = [nu * x_ref[:, s], None, w2_ref[:, s], w3_ref[:, s], None]
        w[1] = tau * (y_ref[:, s] - sigma * w[0])
        w[4] = tau * (total - sigma * w[3])
        for p, (i, j) in enumerate(PAIRS):
            sums[p] = sums[p] + jnp.sum(w[i] * w[j], axis=0, keepdims=True)
    for p in range(len(PAIRS)):
        out_ref[p : p + 1, :] = jnp.broadcast_to(jnp.sum(sums[p], axis=1, keepdims=True), (1, 128))
    for p in range(len(PAIRS), ROWS):
        out_ref[p : p + 1, :] = jnp.zeros((1, 128), jnp.float32)


def gram_rows(scales, quarters, parts, spins):
    return pl.pallas_call(
        functools.partial(gram_kernel, spins, len(parts)),
        out_shape=jax.ShapeDtypeStruct((ROWS, 128), jnp.float32),
        compiler_params=params(),
    )(scales, *quarters, *parts)


def weights_kernel(step_size, scale_ref, sums_ref, out_ref):
    sigma, tau, nu = scale_ref[0:1], scale_ref[1:2], scale_ref[2:3]
    gram = {}
    for p, (i, j) in enumerate(PAIRS):
        gram[(i, j)] = sums_ref[p : p + 1, :]
    low = {}
    inverse = []
    for j in range(4):
        pivot = gram[(j, j)]
        for k in range(j):
            pivot = pivot - low[(j, k)] * low[(j, k)]
        low[(j, j)] = jnp.sqrt(pivot)
        inverse.append(1.0 / low[(j, j)])
        for i in range(j + 1, 5):
            value = gram[(j, i)]
            for k in range(j):
                value = value - low[(i, k)] * low[(j, k)]
            low[(i, j)] = value * inverse[j]
    stretch = 1.0 / tau
    beta = [low[(j + 1, j + 1)] * inverse[j] * stretch for j in range(3)]
    alpha = []
    for j in range(4):
        value = low[(j + 1, j)] * stretch
        if j > 0:
            value = value - low[(j, j - 1)] * beta[j - 1]
        alpha.append(sigma + value * inverse[j])
    factor = step_size / 16.0
    diag = [factor * a for a in alpha]
    off = [factor * b for b in beta]
    one = jnp.ones_like(sigma)
    zero = jnp.zeros_like(sigma)
    result = {(i, j): one if i == j else zero for i in range(4) for j in range(i, 4)}

    def entry(table, i, j):
        return table[(min(i, j), max(i, j))]

    for degree in range(8, 0, -1):
        fresh = {}
        for i in range(4):
            for j in range(i, 4):
                value = diag[i] * entry(result, i, j)
                if i > 0:
                    value = value + off[i - 1] * entry(result, i - 1, j)
                if i < 3:
                    value = value + off[i] * entry(result, i + 1, j)
                value = value * (1.0 / degree)
                fresh[(i, j)] = one + value if i == j else value
        result = fresh
    for squaring in range(4):
        fresh = {}
        for i in range(4):
            for j in range(i, 4):
                if squaring == 3 and i > 0:
                    continue
                value = entry(result, i, 0) * entry(result, 0, j)
                for k in range(1, 4):
                    value = value + entry(result, i, k) * entry(result, k, j)
                fresh[(i, j)] = value
        result = fresh
    column = [result[(0, j)] for j in range(4)]
    size = jnp.sqrt(sum(c * c for c in column))
    c = [None] * 4
    for i in range(3, -1, -1):
        value = column[i]
        for j in range(i + 1, 4):
            value = value - low[(j, i)] * c[j]
        c[i] = value * inverse[i]
    norm = low[(0, 0)] / nu
    c = [norm * v for v in c]
    rows = [(c[0] - c[1] * tau * sigma) * nu, c[1] * tau, c[2], c[3], 1.0 / (norm * size)]
    for p, value in enumerate(rows):
        out_ref[p : p + 1, :] = value
    for p in range(len(rows), 8):
        out_ref[p : p + 1, :] = zero


def basis_weights(scales, sums, step_size):
    return pl.pallas_call(
        functools.partial(weights_kernel, step_size),
        out_shape=jax.ShapeDtypeStruct((8, 128), jnp.float32),
        compiler_params=params(),
    )(scales, sums)


def result_kernel(spins, weight_ref, x_ref, y_ref, w2_ref, w3_ref, out_ref):
    size = out_ref.shape[2]
    for s in range(spins):
        value = weight_ref[0:1, 0:1] * x_ref[:, s * size : (s + 1) * size]
        value = value + weight_ref[1:2, 0:1] * y_ref[s]
        value = value + weight_ref[2:3, 0:1] * w2_ref[s]
        out_ref[s] = value + weight_ref[3:4, 0:1] * w3_ref[s]


def weighted(weights, x, y, w2, w3, spins):
    size = x.shape[0]
    step = 128
    state = pl.BlockSpec((spins, step, size), lambda i: (0, i, 0))
    return pl.pallas_call(
        functools.partial(result_kernel, spins),
        grid=(size // step,),
        in_specs=[
            pl.BlockSpec((8, 128), lambda i: (0, 0)),
            pl.BlockSpec((step, spins * size), lambda i: (i, 0)),
        ]
        + [state] * 3,
        out_specs=state,
        out_shape=jax.ShapeDtypeStruct((spins, size, size), jnp.float32),
        compiler_params=params(),
    )(weights, x, y, w2, w3)


def quarter_state(state, offset, width):
    return jnp.swapaxes(lax.dynamic_slice_in_dim(state, offset, width, 2), 0, 1)


def evolve(x, nu, apply_full, apply_quarter, step_size, spins, offset, width):
    size = x.shape[0]
    blocks = [x[:, s * size : (s + 1) * size] for s in range(spins)]
    parts, _ = apply_full(blocks, None)
    y, sums = first_combine(x, nu, parts, spins)
    parts, totals = apply_full([y[s] for s in range(spins)], sums)
    scales = shift_rows(nu, totals)
    w2 = combine(scales, y, x, parts, spins)
    parts, _ = apply_full([w2[s] for s in range(spins)], None)
    w3 = combine(scales, w2, None, parts, spins)
    parts = apply_quarter([w3[s] for s in range(spins)])
    x_quarter = lax.dynamic_slice_in_dim(x.reshape(size, spins, size), offset, width, 2)
    quarters = [x_quarter] + [quarter_state(w, offset, width) for w in (y, w2, w3)]
    rows = gram_rows(scales, quarters, parts, spins)
    total = sum_over_col(jnp.sum(exchange(rows, "sec"), axis=0))
    weights = basis_weights(scales, total, step_size)
    return weighted(weights, x, y, w2, w3, spins), weights


def body(site_tensor, left_env, right_env, bond_env, sector_sizes):
    col_rows = site_tensor.shape[0]
    size = left_env.shape[2]
    sector = lax.axis_index("sec")
    last = lax.axis_size("sec") - 1
    offset = lax.axis_index("col") * col_rows

    left = left_env[0]
    site_block = site_tensor[:, 0]
    site_full = gather_col(site_block, 0)
    right = gather_col(right_env[0], 2)
    site_nu = inverse_norm(exchange(norm_rows(site_block), ("col", "sec")))

    below_sum = to_next(left[0] + left[1] + ANISOTROPY * left[4])
    below_four = to_next(left[4])
    above_sum = to_previous(left[0] - left[1] + ANISOTROPY * left[4])
    above_four = to_previous(left[4])
    raise_here = jnp.where(sector < last, ROOT_TWO * left[2], 0.0)
    lower_here = jnp.where(sector > 0, ROOT_TWO * left[3], 0.0)
    right_plus = right[4] + right[1]
    right_minus = right[4] - right[1]
    half = ROOT_TWO / 2
    up_matrix = half * right[2].T
    down_matrix = half * right[3].T

    lefts = dict(
        bs=below_sum, b4=below_four, us=above_sum, u4=above_four, h4=left[4], h0=left[0],
        low=lower_here, lowt=lower_here.T, rai=raise_here, rait=raise_here.T,
    )
    lefts_quarter = {k: lax.dynamic_slice_in_dim(v, offset, col_rows, 1) for k, v in lefts.items()}

    def apply_site(env, blocks, sums):
        x0, x1, x2 = blocks
        z1 = mm(x1, env["h4"])
        send_down1 = mm(down_matrix, z1)
        send_up1 = mm(up_matrix, z1)
        above1 = to_previous(send_down1)
        below1 = to_next(send_up1)
        z0 = mm(x0, env["b4"])
        above0 = to_previous(mm(down_matrix, z0))
        z2 = mm(x2, env["u4"])
        send_up2 = mm(up_matrix, z2)
        below2 = to_next(send_up2)
        totals = None
        if sums is not None:
            sums, _ = lax.optimization_barrier((sums, send_up2))
            totals = exchange(sums, "sec")
        p0 = mm(x0, env["bs"]) + mm(x1, env["low"])
        p1 = mm(x1, env["h0"]) + mm(x0, env["lowt"]) + mm(x2, env["rait"])
        p2 = mm(x2, env["us"]) + mm(x1, env["rai"])
        y0 = mm(right[0], p0) + mm(right_plus, z0)
        y1 = mm(right[0], p1) + mm(right[4], z1)
        y2 = mm(right[0], p2) + mm(right_minus, z2)
        return [y0, below1, y1, below2, above0, y2, above1], totals

    evolved, weights = evolve(
        site_full,
        site_nu,
        lambda blocks, sums: apply_site(lefts, blocks, sums),
        lambda blocks: apply_site(lefts_quarter, blocks, None)[0],
        -TIME_STEP,
        3,
        offset,
        col_rows,
    )
    gram = None
    for s in range(3):
        term = lax.dot_general(
            evolved[s], evolved[s], (((1,), (1,)), ((), ())), precision=HIGHEST
        )
        gram = term if gram is None else gram + term
    live = (jnp.arange(size) < sector_sizes[0]).astype(jnp.float32)
    gram = gram + (1.0 - live)[:, None] * jnp.eye(size, dtype=jnp.float32)
    factor = jnp.linalg.cholesky(gram[None])[0]
    bond_scale = math.sqrt(3.0 * size)
    start = factor * live[:, None] * live[None, :] / bond_scale
    bond_nu = jnp.broadcast_to(weights[4:5] * bond_scale, (8, 128))

    bond = bond_env[0]
    bonds = dict(dn=ROOT_TWO * bond[3], up=ROOT_TWO * bond[2], b0=bond[0], b1=bond[1], b4=bond[4])
    bonds_quarter = {k: lax.dynamic_slice_in_dim(v, offset, col_rows, 1) for k, v in bonds.items()}

    def apply_bond(env, blocks, sums):
        (x,) = blocks
        from_above = to_previous(mm(down_matrix, mm(x, env["dn"])))
        send_up = mm(up_matrix, mm(x, env["up"]))
        from_below = to_next(send_up)
        totals = None
        if sums is not None:
            sums, _ = lax.optimization_barrier((sums, send_up))
            totals = exchange(sums, "sec")
        y = mm(right[0], mm(x, env["b0"]))
        y = y + mm(right[1], mm(x, env["b1"]))
        y = y + mm(right[4], mm(x, env["b4"]))
        return [y, from_above, from_below], totals

    evolved_bond, _ = evolve(
        start,
        bond_nu,
        lambda blocks, sums: apply_bond(bonds, blocks, sums),
        lambda blocks: apply_bond(bonds_quarter, blocks, None)[0],
        TIME_STEP,
        1,
        offset,
        col_rows,
    )

    out_site = jnp.swapaxes(lax.dynamic_slice_in_dim(evolved, offset, col_rows, 1), 0, 1)
    out_site = out_site.reshape(col_rows, 1, 3 * size)
    out_bond = lax.dynamic_slice_in_dim(evolved_bond[0], offset, col_rows, 0)[:, None, :]
    return (out_site, out_bond)


def solution(mesh):
    in_specs = (
        P("col", "sec", None),
        P("sec", None, None, None),
        P("sec", None, None, "col"),
        P("sec", None, None, None),
        P("sec"),
    )
    out_specs = (P("col", "sec", None), P("col", "sec", None))
    return jax.shard_map(body, mesh=mesh, in_specs=in_specs, out_specs=out_specs, check_vma=False)
```

```python
import functools
import math

import jax
import jax.numpy as jnp
from jax import lax
from jax.experimental import pallas as pl
from jax.experimental.pallas import tpu as pltpu
from jax.sharding import PartitionSpec as P

KRYLOV = 4
HIGHEST = lax.Precision.HIGHEST
HIGH = lax.Precision.HIGH
ROOT_TWO = math.sqrt(2.0)
ANISOTROPY = 0.5
TIME_STEP = 0.1
VMEM_LIMIT = 48 * 1024 * 1024


def to_next(block):
    count = lax.axis_size("sec")
    return lax.ppermute(block, "sec", [(i, i + 1) for i in range(count - 1)])


def to_previous(block):
    count = lax.axis_size("sec")
    return lax.ppermute(block, "sec", [(i + 1, i) for i in range(count - 1)])


def gather_col(block, axis):
    return lax.all_gather(block, "col", axis=axis, tiled=True)


def mm(left, right):
    return jnp.dot(left, right, precision=HIGH)


def params():
    return pltpu.CompilerParams(vmem_limit_bytes=VMEM_LIMIT)


def exchange(rows, axis):
    count = lax.axis_size(axis) if isinstance(axis, str) else lax.axis_size(axis[0]) * lax.axis_size(axis[1])
    sent = jnp.broadcast_to(rows[None], (count,) + rows.shape)
    return lax.all_to_all(sent, axis, 0, 0)


def row_of(values, shape):
    lane = lax.broadcasted_iota(jnp.int32, shape, 1)
    row = lax.broadcasted_iota(jnp.int32, shape, 0)
    out = jnp.zeros(shape, jnp.float32)
    for p, value in enumerate(values):
        out = jnp.where((lane == p) & (row == 0), value, out)
    return out


def spin_parts(spins, s):
    if spins == 1:
        return range(3)
    return range((2, 3, 2)[s])


def add_parts(spins, part_refs):
    totals = []
    index = 0
    for s in range(spins):
        total = None
        for part in spin_parts(spins, s):
            value = part_refs[index][...]
            index += 1
            total = value if total is None else total + value
        totals.append(total)
    return totals


SCALARS = jax.ShapeDtypeStruct((8, 128), jnp.float32)


def scalar_spec():
    return pl.BlockSpec((8, 128), lambda *i: (0, 0))


def norm_kernel(a_ref, out_ref):
    a = a_ref[...]
    out_ref[...] = row_of([jnp.sum(a * a)], out_ref.shape)


def norm_row(block):
    return pl.pallas_call(norm_kernel, out_shape=SCALARS, compiler_params=params())(block)


def inverse_norm_kernel(parts_ref, out_ref):
    total = jnp.sum(parts_ref[...], axis=0)
    out_ref[...] = jnp.broadcast_to(1.0 / jnp.sqrt(total[0:1, 0:1]), out_ref.shape)


def inverse_norm(parts):
    return pl.pallas_call(inverse_norm_kernel, out_shape=SCALARS, compiler_params=params())(parts)


def x_specs(spins, step, size):
    return [pl.BlockSpec((step, size), functools.partial(lambda s, i: (i, s), s)) for s in range(spins)]


def first_combine_kernel(spins, count, *refs):
    scale_ref, x_refs = refs[0], refs[1 : 1 + spins]
    part_refs = refs[1 + spins : 1 + spins + count]
    y_refs, sums_ref = refs[1 + spins + count : -1], refs[-1]
    nu = scale_ref[2:3, 0:1]
    cross = jnp.float32(0.0)
    square = jnp.float32(0.0)
    for s, total in enumerate(add_parts(spins, part_refs)):
        y = total * nu
        y_refs[s][...] = y
        cross += jnp.sum(x_refs[s][...] * nu * y)
        square += jnp.sum(y * y)

    @pl.when(pl.program_id(0) == 0)
    def _():
        sums_ref[...] = jnp.zeros_like(sums_ref)

    sums_ref[...] += row_of([cross, square], sums_ref.shape)


def first_combine(x, nu, parts, spins):
    size = x.shape[0]
    step = 128
    spec = pl.BlockSpec((step, size), lambda i: (i, 0))
    *y, sums = pl.pallas_call(
        functools.partial(first_combine_kernel, spins, len(parts)),
        grid=(size // step,),
        in_specs=[scalar_spec()] + x_specs(spins, step, size) + [spec] * len(parts),
        out_specs=[spec] * spins + [scalar_spec()],
        out_shape=[jax.ShapeDtypeStruct((size, size), jnp.float32)] * spins + [SCALARS],
        compiler_params=params(),
    )(nu, *([x] * spins), *parts)
    return y, sums


def shift_kernel(nu_ref, parts_ref, out_ref):
    total = jnp.sum(parts_ref[...], axis=0)
    row = lax.broadcasted_iota(jnp.int32, out_ref.shape, 0)
    sigma = total[0:1, 0:1]
    tau = 1.0 / jnp.sqrt(total[0:1, 1:2])
    out_ref[...] = jnp.where(row == 0, sigma, jnp.where(row == 1, tau, nu_ref[...]))


def shift_rows(nu, parts):
    return pl.pallas_call(shift_kernel, out_shape=SCALARS, compiler_params=params())(nu, parts)


def combine_kernel(second, spins, count, *refs):
    scale_ref = refs[0]
    sigma, tau, nu = scale_ref[0:1, 0:1], scale_ref[1:2, 0:1], scale_ref[2:3, 0:1]
    w_refs = refs[1 : 1 + spins]
    base = 1 + spins
    if second:
        x_refs = refs[base : base + spins]
        base += spins
    part_refs = refs[base : base + count]
    out_refs = refs[base + count :]
    for s, total in enumerate(add_parts(spins, part_refs)):
        w = w_refs[s][...]
        if second:
            inner = w - sigma * (nu * x_refs[s][...])
            out_refs[s][...] = tau * tau * ((total - sigma * w) - sigma * inner)
        else:
            out_refs[s][...] = tau * (total - sigma * w)


def combine(scales, w, x, parts, spins):
    size = w[0].shape[1]
    step = 128
    spec = pl.BlockSpec((step, size), lambda i: (i, 0))
    second = x is not None
    return pl.pallas_call(
        functools.partial(combine_kernel, second, spins, len(parts)),
        grid=(size // step,),
        in_specs=[scalar_spec()]
        + [spec] * spins
        + (x_specs(spins, step, size) if second else [])
        + [spec] * len(parts),
        out_specs=[spec] * spins,
        out_shape=[jax.ShapeDtypeStruct((size, size), jnp.float32)] * spins,
        compiler_params=params(),
    )(scales, *w, *([x] * spins if second else []), *parts)


PAIRS = [(i, j) for j in range(5) for i in range(j + 1) if (i, j) != (4, 4)]


def gram_kernel(spins, count, place_ref, *refs):
    scale_ref = refs[0]
    bases = [refs[1 + k * spins : 1 + (k + 1) * spins] for k in range(4)]
    part_refs = refs[1 + 4 * spins : 1 + 4 * spins + count]
    out_ref = refs[-1]
    sigma, tau, nu = scale_ref[0:1, 0:1], scale_ref[1:2, 0:1], scale_ref[2:3, 0:1]
    sums = [jnp.zeros((8, 128), jnp.float32)] * len(PAIRS)
    chunk = 64
    size = part_refs[0].shape[0]
    for start in range(0, size, chunk):
        index = 0
        for s in range(spins):
            total = None
            for part in spin_parts(spins, s):
                value = part_refs[index][start : start + chunk, :]
                index += 1
                total = value if total is None else total + value
            x, y, w2, w3 = (bases[k][s][start : start + chunk, :] for k in range(4))
            w = [nu * x, None, w2, w3, None]
            w[1] = tau * (y - sigma * w[0])
            w[4] = tau * (total - sigma * w[3])
            for p, (i, j) in enumerate(PAIRS):
                product = (w[i] * w[j]).reshape(chunk // 8, 8, 128)
                sums[p] = sums[p] + jnp.sum(product, axis=0)
    out_ref[...] = row_of([jnp.sum(value) for value in sums], out_ref.shape)


def gram_row(place, scales, x, states, parts, spins):
    size = x.shape[0]
    width = parts[0].shape[1]
    per = size // width

    x_quarter = [
        pl.BlockSpec((size, width), functools.partial(lambda s, i, p: (0, s * per + p[0]), s))
        for s in range(spins)
    ]
    quarter = pl.BlockSpec((size, width), lambda i, p: (0, p[0]))
    whole = pl.BlockSpec((size, width), lambda i, p: (0, 0))
    flat = [w for state in states for w in state]
    return pl.pallas_call(
        functools.partial(gram_kernel, spins, len(parts)),
        grid_spec=pltpu.PrefetchScalarGridSpec(
            num_scalar_prefetch=1,
            grid=(1,),
            in_specs=[scalar_spec()] + x_quarter + [quarter] * len(flat) + [whole] * len(parts),
            out_specs=scalar_spec(),
        ),
        out_shape=SCALARS,
        compiler_params=params(),
    )(place, scales, *([x] * spins), *flat, *parts)


def weights_kernel(step_size, scale_ref, sums_ref, out_ref):
    sigma, tau, nu = scale_ref[0:1], scale_ref[1:2], scale_ref[2:3]
    total = jnp.sum(sums_ref[...], axis=0)[0:1]
    gram = {}
    for p, (i, j) in enumerate(PAIRS):
        gram[(i, j)] = jnp.broadcast_to(total[:, p : p + 1], (1, 128))
    low = {}
    inverse = []
    for j in range(4):
        pivot = gram[(j, j)]
        for k in range(j):
            pivot = pivot - low[(j, k)] * low[(j, k)]
        low[(j, j)] = jnp.sqrt(pivot)
        inverse.append(1.0 / low[(j, j)])
        for i in range(j + 1, 5):
            value = gram[(j, i)]
            for k in range(j):
                value = value - low[(i, k)] * low[(j, k)]
            low[(i, j)] = value * inverse[j]
    stretch = 1.0 / tau
    beta = [low[(j + 1, j + 1)] * inverse[j] * stretch for j in range(3)]
    alpha = []
    for j in range(4):
        value = low[(j + 1, j)] * stretch
        if j > 0:
            value = value - low[(j, j - 1)] * beta[j - 1]
        alpha.append(sigma + value * inverse[j])
    factor = step_size / 16.0
    diag = [factor * a for a in alpha]
    off = [factor * b for b in beta]
    one = jnp.ones_like(sigma)
    zero = jnp.zeros_like(sigma)
    result = {(i, j): one if i == j else zero for i in range(4) for j in range(i, 4)}

    def entry(table, i, j):
        return table[(min(i, j), max(i, j))]

    for degree in range(8, 0, -1):
        fresh = {}
        for i in range(4):
            for j in range(i, 4):
                value = diag[i] * entry(result, i, j)
                if i > 0:
                    value = value + off[i - 1] * entry(result, i - 1, j)
                if i < 3:
                    value = value + off[i] * entry(result, i + 1, j)
                value = value * (1.0 / degree)
                fresh[(i, j)] = one + value if i == j else value
        result = fresh
    for squaring in range(4):
        fresh = {}
        for i in range(4):
            for j in range(i, 4):
                if squaring == 3 and i > 0:
                    continue
                value = entry(result, i, 0) * entry(result, 0, j)
                for k in range(1, 4):
                    value = value + entry(result, i, k) * entry(result, k, j)
                fresh[(i, j)] = value
        result = fresh
    column = [result[(0, j)] for j in range(4)]
    size = jnp.sqrt(sum(c * c for c in column))
    c = [None] * 4
    for i in range(3, -1, -1):
        value = column[i]
        for j in range(i + 1, 4):
            value = value - low[(j, i)] * c[j]
        c[i] = value * inverse[i]
    norm = low[(0, 0)] / nu
    c = [norm * v for v in c]
    rows = [(c[0] - c[1] * tau * sigma) * nu, c[1] * tau, c[2], c[3], 1.0 / (norm * size)]
    for p, value in enumerate(rows):
        out_ref[p : p + 1, :] = value
    for p in range(len(rows), 8):
        out_ref[p : p + 1, :] = zero


def basis_weights(scales, sums, step_size):
    return pl.pallas_call(
        functools.partial(weights_kernel, step_size),
        out_shape=SCALARS,
        compiler_params=params(),
    )(scales, sums)


def result_kernel(spins, *refs):
    weight_ref = refs[0]
    bases = [refs[1 + k * spins : 1 + (k + 1) * spins] for k in range(4)]
    out_refs = refs[1 + 4 * spins :]
    for s in range(spins):
        value = weight_ref[0:1, 0:1] * bases[0][s][...]
        for k in range(1, 4):
            value = value + weight_ref[k : k + 1, 0:1] * bases[k][s][...]
        out_refs[s][...] = value


def weighted(weights, x, states, spins):
    size = x.shape[0]
    step = 128
    spec = pl.BlockSpec((step, size), lambda i: (i, 0))
    flat = [w for state in states for w in state]
    return pl.pallas_call(
        functools.partial(result_kernel, spins),
        grid=(size // step,),
        in_specs=[scalar_spec()] + x_specs(spins, step, size) + [spec] * len(flat),
        out_specs=[spec] * spins,
        out_shape=[jax.ShapeDtypeStruct((size, size), jnp.float32)] * spins,
        compiler_params=params(),
    )(weights, *([x] * spins), *flat)


def output_kernel(spins, place_ref, *refs):
    weight_ref = refs[0]
    bases = [refs[1 + k * spins : 1 + (k + 1) * spins] for k in range(4)]
    out_ref = refs[1 + 4 * spins]
    size = bases[0][0].shape[1]
    for s in range(spins):
        value = weight_ref[0:1, 0:1] * bases[0][s][...]
        for k in range(1, 4):
            value = value + weight_ref[k : k + 1, 0:1] * bases[k][s][...]
        out_ref[:, s * size : (s + 1) * size] = value


def output_rows(place, weights, x, states, spins, rows):
    size = x.shape[0]
    x_rows = [
        pl.BlockSpec((rows, size), functools.partial(lambda s, i, p: (p[0], s), s))
        for s in range(spins)
    ]
    spec = pl.BlockSpec((rows, size), lambda i, p: (p[0], 0))
    flat = [w for state in states for w in state]
    return pl.pallas_call(
        functools.partial(output_kernel, spins),
        grid_spec=pltpu.PrefetchScalarGridSpec(
            num_scalar_prefetch=1,
            grid=(1,),
            in_specs=[scalar_spec()] + x_rows + [spec] * len(flat),
            out_specs=pl.BlockSpec((rows, spins * size), lambda i, p: (0, 0)),
        ),
        out_shape=jax.ShapeDtypeStruct((rows, spins * size), jnp.float32),
        compiler_params=params(),
    )(place, weights, *([x] * spins), *flat)


def evolve(place, x, nu, apply_full, apply_quarter, step_size, spins):
    size = x.shape[0]
    parts, _ = apply_full([x[:, s * size : (s + 1) * size] for s in range(spins)], None)
    y, sums = first_combine(x, nu, parts, spins)
    parts, totals = apply_full(y, sums)
    scales = shift_rows(nu, totals)
    w2 = combine(scales, y, x, parts, spins)
    parts, _ = apply_full(w2, None)
    w3 = combine(scales, w2, None, parts, spins)
    parts = apply_quarter(w3)
    states = [y, w2, w3]
    row = gram_row(place, scales, x, states, parts, spins)
    weights = basis_weights(scales, exchange(row, ("col", "sec")), step_size)
    return states, weights


def body(site_tensor, left_env, right_env, bond_env, sector_sizes):
    col_rows = site_tensor.shape[0]
    size = left_env.shape[2]
    sector = lax.axis_index("sec")
    last = lax.axis_size("sec") - 1
    col = lax.axis_index("col")
    place = col.reshape(1).astype(jnp.int32)

    def quarter_of(*matrices):
        picked = [lax.dynamic_slice_in_dim(m, col * col_rows, col_rows, 1) for m in matrices]
        return jnp.concatenate(picked, axis=1)

    def cut(matrix):
        return [matrix[:, i : i + col_rows] for i in range(0, matrix.shape[1], col_rows)]

    def join(*blocks):
        return jnp.concatenate(blocks, axis=1)

    left = left_env[0]
    site_block = site_tensor[:, 0]
    site_full = gather_col(site_block, 0)
    right = gather_col(right_env[0], 2)
    site_nu = inverse_norm(exchange(norm_row(site_block), ("col", "sec")))

    below_sum = to_next(left[0] + left[1] + ANISOTROPY * left[4])
    below_four = to_next(left[4])
    above_sum = to_previous(left[0] - left[1] + ANISOTROPY * left[4])
    above_four = to_previous(left[4])
    raise_here = jnp.where(sector < last, ROOT_TWO * left[2], 0.0)
    lower_here = jnp.where(sector > 0, ROOT_TWO * left[3], 0.0)
    right_plus = right[4] + right[1]
    right_minus = right[4] - right[1]
    half = ROOT_TWO / 2
    up_matrix = half * right[2].T
    down_matrix = half * right[3].T

    lower_turned, raise_turned = lower_here.T, raise_here.T
    quarter_zero = quarter_of(below_sum, below_four, lower_turned)
    quarter_one = quarter_of(left[4], lower_here, left[0], raise_here)
    quarter_two = quarter_of(above_sum, above_four, raise_turned)

    def apply_site(blocks, sums):
        x0, x1, x2 = blocks
        z1 = mm(x1, left[4])
        send_down1 = mm(down_matrix, z1)
        send_up1 = mm(up_matrix, z1)
        above1 = to_previous(send_down1)
        below1 = to_next(send_up1)
        z0 = mm(x0, below_four)
        above0 = to_previous(mm(down_matrix, z0))
        z2 = mm(x2, above_four)
        send_up2 = mm(up_matrix, z2)
        below2 = to_next(send_up2)
        totals = None
        if sums is not None:
            sums, _ = lax.optimization_barrier((sums, send_up2))
            totals = exchange(sums, "sec")
        p0 = mm(x0, below_sum) + mm(x1, lower_here)
        p1 = mm(x1, left[0]) + mm(x0, lower_turned) + mm(x2, raise_turned)
        p2 = mm(x2, above_sum) + mm(x1, raise_here)
        y0 = mm(right[0], p0) + mm(right_plus, z0)
        y1 = mm(right[0], p1) + mm(right[4], z1)
        y2 = mm(right[0], p2) + mm(right_minus, z2)
        return [y0, below1, y1, below2, above0, y2, above1], totals

    def apply_site_quarter(blocks):
        x0, x1, x2 = blocks
        p0, z0, p1 = cut(mm(x0, quarter_zero))
        z1, more0, more1, p2 = cut(mm(x1, quarter_one))
        last2, z2, last1 = cut(mm(x2, quarter_two))
        above = to_previous(mm(down_matrix, join(z0, z1)))
        below = to_next(mm(up_matrix, join(z1, z2)))
        y0, y1, y2 = cut(mm(right[0], join(p0 + more0, p1 + more1 + last1, p2 + last2)))
        y0 = y0 + mm(right_plus, z0)
        y1 = y1 + mm(right[4], z1)
        y2 = y2 + mm(right_minus, z2)
        above0, above1 = cut(above)
        below1, below2 = cut(below)
        return [y0, below1, y1, below2, above0, y2, above1]

    states, weights = evolve(
        place, site_full, site_nu, apply_site, apply_site_quarter, -TIME_STEP, 3
    )
    evolved = weighted(weights, site_full, states, 3)
    out_site = output_rows(place, weights, site_full, states, 3, col_rows)[:, None, :]
    gram = None
    for s in range(3):
        term = lax.dot_general(
            evolved[s], evolved[s], (((1,), (1,)), ((), ())), precision=HIGHEST
        )
        gram = term if gram is None else gram + term
    live = (jnp.arange(size) < sector_sizes[0]).astype(jnp.float32)
    gram = gram + (1.0 - live)[:, None] * jnp.eye(size, dtype=jnp.float32)
    factor = jnp.linalg.cholesky(gram[None])[0]
    bond_scale = math.sqrt(3.0 * size)
    start = factor * live[:, None] * live[None, :] / bond_scale
    bond_nu = jnp.broadcast_to(weights[4:5] * bond_scale, (8, 128))

    bond = bond_env[0]
    down_bond, up_bond = ROOT_TWO * bond[3], ROOT_TWO * bond[2]
    quarter_bond = quarter_of(down_bond, up_bond, bond[0], bond[1], bond[4])

    def apply_bond(blocks, sums):
        (x,) = blocks
        from_above = to_previous(mm(down_matrix, mm(x, down_bond)))
        send_up = mm(up_matrix, mm(x, up_bond))
        from_below = to_next(send_up)
        totals = None
        if sums is not None:
            sums, _ = lax.optimization_barrier((sums, send_up))
            totals = exchange(sums, "sec")
        y = mm(right[0], mm(x, bond[0]))
        y = y + mm(right[1], mm(x, bond[1]))
        y = y + mm(right[4], mm(x, bond[4]))
        return [y, from_above, from_below], totals

    def apply_bond_quarter(blocks):
        down, up, m0, m1, m4 = cut(mm(blocks[0], quarter_bond))
        from_above = to_previous(mm(down_matrix, down))
        from_below = to_next(mm(up_matrix, up))
        y = mm(right[0], m0) + mm(right[1], m1) + mm(right[4], m4)
        return [y, from_above, from_below]

    states, weights = evolve(place, start, bond_nu, apply_bond, apply_bond_quarter, TIME_STEP, 1)
    out_bond = output_rows(place, weights, start, states, 1, col_rows)[:, None, :]
    return (out_site, out_bond)


def solution(mesh):
    in_specs = (
        P("col", "sec", None),
        P("sec", None, None, None),
        P("sec", None, None, "col"),
        P("sec", None, None, None),
        P("sec"),
    )
    out_specs = (P("col", "sec", None), P("col", "sec", None))
    return jax.shard_map(body, mesh=mesh, in_specs=in_specs, out_specs=out_specs, check_vma=False)
```

```python
import functools
import math

import jax
import jax.numpy as jnp
from jax import lax
from jax.experimental import pallas as pl
from jax.experimental.pallas import tpu as pltpu
from jax.sharding import PartitionSpec as P

KRYLOV = 4
HIGHEST = lax.Precision.HIGHEST
ROOT_TWO = math.sqrt(2.0)
ANISOTROPY = 0.5
TIME_STEP = 0.1
VMEM_LIMIT = 48 * 1024 * 1024


def to_next(block):
    count = lax.axis_size("sec")
    return lax.ppermute(block, "sec", [(i, i + 1) for i in range(count - 1)])


def to_previous(block):
    count = lax.axis_size("sec")
    return lax.ppermute(block, "sec", [(i + 1, i) for i in range(count - 1)])


def gather_col(block, axis):
    return lax.all_gather(block, "col", axis=axis, tiled=True)


def params():
    return pltpu.CompilerParams(vmem_limit_bytes=VMEM_LIMIT)


def exchange(rows, axis):
    count = lax.axis_size(axis) if isinstance(axis, str) else lax.axis_size(axis[0]) * lax.axis_size(axis[1])
    sent = jnp.broadcast_to(rows[None], (count,) + rows.shape)
    return lax.all_to_all(sent, axis, 0, 0)


def row_of(values, shape):
    lane = lax.broadcasted_iota(jnp.int32, shape, 1)
    row = lax.broadcasted_iota(jnp.int32, shape, 0)
    out = jnp.zeros(shape, jnp.float32)
    for p, value in enumerate(values):
        out = jnp.where((lane == p) & (row == 0), value, out)
    return out


def add_parts(spins, part_refs, rows=slice(None)):
    local = part_refs[0]
    if spins == 1:
        return [local[0, rows, :] + part_refs[1][rows, :] + part_refs[2][rows, :]]
    down0, down1, up1, up2 = (ref[rows, :] for ref in part_refs[1:])
    return [local[0, rows, :] + up1, local[1, rows, :] + (up2 + down0), local[2, rows, :] + down1]


BF16 = jnp.bfloat16


def split(value):
    high = value.astype(BF16)
    return high, (value - high.astype(jnp.float32)).astype(BF16)


def product(left, right):
    def dot(a, b):
        return jnp.dot(a, b, preferred_element_type=jnp.float32)

    return dot(left[0], right[0]) + (dot(left[0], right[1]) + dot(left[1], right[0]))


SCALARS = jax.ShapeDtypeStruct((8, 128), jnp.float32)


def scalar_spec():
    return pl.BlockSpec((8, 128), lambda *i: (0, 0))


def norm_kernel(a_ref, out_ref):
    a = a_ref[...]
    out_ref[...] = row_of([jnp.sum(a * a)], out_ref.shape)


def norm_row(block):
    return pl.pallas_call(norm_kernel, out_shape=SCALARS, compiler_params=params())(block)


def inverse_norm_kernel(parts_ref, out_ref):
    total = jnp.sum(parts_ref[...], axis=0)
    out_ref[...] = jnp.broadcast_to(1.0 / jnp.sqrt(total[0:1, 0:1]), out_ref.shape)


def inverse_norm(parts):
    return pl.pallas_call(inverse_norm_kernel, out_shape=SCALARS, compiler_params=params())(parts)


def split_kernel(x_ref, high_ref, low_ref):
    high_ref[...], low_ref[...] = split(x_ref[...])


def split_state(x):
    rows, columns = x.shape
    step = 128
    spec = pl.BlockSpec((step, columns), lambda i: (i, 0))
    return pl.pallas_call(
        split_kernel,
        grid=(rows // step,),
        in_specs=[spec],
        out_specs=[spec] * 2,
        out_shape=[jax.ShapeDtypeStruct((rows, columns), BF16)] * 2,
        compiler_params=params(),
    )(x)


def right_kernel(block_ref, stack_ref, up_ref, down_ref):
    r0, r1, r2, r3, r4 = (block_ref[0, b] for b in range(5))
    for k, value in enumerate((r0, r4 + r1, r4, r4 - r1, r1)):
        stack_ref[k, 0], stack_ref[k, 1] = split(value)
    half = ROOT_TWO / 2
    up_ref[0], up_ref[1] = split(half * r2.T)
    down_ref[0], down_ref[1] = split(half * r3.T)


def right_parts(blocks):
    count, _, size, width = blocks.shape
    turned = pl.BlockSpec((2, width, size), lambda i: (0, i, 0))
    pair = jax.ShapeDtypeStruct((2, size, size), BF16)
    return pl.pallas_call(
        right_kernel,
        grid=(count,),
        in_specs=[pl.BlockSpec((1, 5, size, width), lambda i: (i, 0, 0, 0))],
        out_specs=[pl.BlockSpec((5, 2, size, width), lambda i: (0, 0, 0, i)), turned, turned],
        out_shape=[jax.ShapeDtypeStruct((5, 2, size, size), BF16), pair, pair],
        compiler_params=params(),
    )(blocks)


def left_kernel(flag_ref, left_ref, bsum_ref, bfour_ref, asum_ref, afour_ref, four_ref, mix_ref):
    has_above, has_below = flag_ref[0], flag_ref[1]
    for k, value in enumerate((bfour_ref[...], left_ref[4], afour_ref[...])):
        four_ref[k, 0], four_ref[k, 1] = split(value)
    raise_here = jnp.where(has_above > 0, ROOT_TWO * left_ref[2], 0.0)
    lower_here = jnp.where(has_below > 0, ROOT_TWO * left_ref[3], 0.0)
    mixes = (
        bsum_ref[...], lower_here, left_ref[0], lower_here.T, raise_here.T, asum_ref[...], raise_here
    )
    for k, value in enumerate(mixes):
        mix_ref[k, 0], mix_ref[k, 1] = split(value)


def left_parts(flags, left, below_sum, below_four, above_sum, above_four):
    size = left.shape[1]
    vmem = pl.BlockSpec(memory_space=pltpu.VMEM)
    return pl.pallas_call(
        left_kernel,
        in_specs=[pl.BlockSpec(memory_space=pltpu.SMEM)] + [vmem] * 5,
        out_specs=[vmem] * 2,
        out_shape=[
            jax.ShapeDtypeStruct((3, 2, size, size), BF16),
            jax.ShapeDtypeStruct((7, 2, size, size), BF16),
        ],
        compiler_params=params(),
    )(flags, left, below_sum, below_four, above_sum, above_four)


def bond_kernel(p_ref, out_ref):
    a = pl.program_id(0)
    scale = jnp.where((a == 2) | (a == 3), ROOT_TWO, 1.0).astype(jnp.float32)
    out_ref[0, 0], out_ref[0, 1] = split(scale * p_ref[0])


def bond_parts(bond):
    count, size, _ = bond.shape
    return pl.pallas_call(
        bond_kernel,
        grid=(count,),
        in_specs=[pl.BlockSpec((1, size, size), lambda i: (i, 0, 0))],
        out_specs=pl.BlockSpec((1, 2, size, size), lambda i: (i, 0, 0, 0)),
        out_shape=jax.ShapeDtypeStruct((count, 2, size, size), BF16),
        compiler_params=params(),
    )(bond)


def pair_of(ref, index):
    return ref[index, 0], ref[index, 1]


def columns_of(high_ref, low_ref, s):
    size = high_ref.shape[0]
    cut = slice(s * size, (s + 1) * size)
    return high_ref[:, cut], low_ref[:, cut]


def site_send_kernel(place_ref, high, low, four_ref, up_ref, down_ref, d0, d1, u1, u2, zh, zl):
    up, down = (up_ref[0], up_ref[1]), (down_ref[0], down_ref[1])
    z = []
    for s in (1, 0, 2):
        pair = split(product(columns_of(high, low, s), pair_of(four_ref, s)))
        zh[s], zl[s] = pair
        if s < 2:
            (d0, d1)[s][...] = product(down, pair)
        if s > 0:
            (u1, u2)[s - 1][...] = product(up, pair)


def site_local_kernel(place_ref, high, low, mix_ref, stack_ref, zh, zl, out_ref):
    x = [columns_of(high, low, s) for s in range(3)]
    terms = (((0, 0), (1, 1)), ((1, 2), (0, 3), (2, 4)), ((2, 5), (1, 6)))
    for s in range(3):
        total = None
        for source, matrix in terms[s]:
            value = product(x[source], pair_of(mix_ref, matrix))
            total = value if total is None else total + value
        y = product(pair_of(stack_ref, 0), split(total))
        out_ref[s] = y + product(pair_of(stack_ref, 1 + s), (zh[s], zl[s]))


def bond_send_kernel(place_ref, high, low, p_ref, up_ref, down_ref, d_ref, u_ref):
    x = (high[...], low[...])
    d_ref[...] = product((down_ref[0], down_ref[1]), split(product(x, pair_of(p_ref, 3))))
    u_ref[...] = product((up_ref[0], up_ref[1]), split(product(x, pair_of(p_ref, 2))))


def bond_local_kernel(place_ref, high, low, p_ref, stack_ref, out_ref):
    x = (high[...], low[...])
    total = None
    for a, matrix in ((0, 0), (4, 2), (1, 4)):
        value = product(pair_of(stack_ref, matrix), split(product(x, pair_of(p_ref, a))))
        total = value if total is None else total + value
    out_ref[0] = total


def product_call(kernel, place, whole, cut, outs, quarter, flops):
    size = cut[0].shape[-1]
    width = size // 4 if quarter else size // 2

    def by_place(array):
        lead = (0,) * (array.ndim - 1)
        block = array.shape[:-1] + (width,)
        if quarter and array.shape[-1] == width:
            return pl.BlockSpec(block, lambda i, p: lead + (0,))
        if quarter:
            return pl.BlockSpec(block, lambda i, p: lead + (p[0],))
        return pl.BlockSpec(block, lambda i, p: lead + (i,))

    def all_of(array):
        lead = (0,) * array.ndim
        return pl.BlockSpec(array.shape, lambda i, p: lead)

    shapes = [
        jax.ShapeDtypeStruct(shape + (size, width if quarter else size), dtype) for shape, dtype in outs
    ]
    return pl.pallas_call(
        kernel,
        grid_spec=pltpu.PrefetchScalarGridSpec(
            num_scalar_prefetch=1,
            grid=(1 if quarter else size // width,),
            in_specs=[all_of(a) if is_whole else by_place(a) for is_whole, a in whole],
            out_specs=[by_place(shape) for shape in shapes],
        ),
        out_shape=shapes,
        compiler_params=params(),
        cost_estimate=pl.CostEstimate(
            flops=flops // (4 if quarter else 1), bytes_accessed=16 * 2**20, transcendentals=0
        ),
    )(place, *[a for _, a in whole])


UNIT = 6 * 512**3


def state_spec(spins, step, size):
    return pl.BlockSpec((step, spins * size), lambda i: (i, 0))


def part_specs(spins, step, size, count):
    row = pl.BlockSpec((step, size), lambda i: (i, 0))
    return [pl.BlockSpec((spins, step, size), lambda i: (0, i, 0))] + [row] * (count - 1)


def state_shapes(spins, size):
    full = (size, spins * size)
    return [jax.ShapeDtypeStruct(full, t) for t in (jnp.float32, BF16, BF16)]


def first_combine_kernel(spins, scale_ref, x_ref, *refs):
    part_refs, (y_ref, high_ref, low_ref, sums_ref) = refs[:-4], refs[-4:]
    nu = scale_ref[2:3, 0:1]
    size = part_refs[0].shape[2]
    cross = jnp.float32(0.0)
    square = jnp.float32(0.0)
    for s, total in enumerate(add_parts(spins, part_refs)):
        cut = slice(s * size, (s + 1) * size)
        y = total * nu
        y_ref[:, cut] = y
        high_ref[:, cut], low_ref[:, cut] = split(y)
        cross += jnp.sum(x_ref[:, cut] * nu * y)
        square += jnp.sum(y * y)

    @pl.when(pl.program_id(0) == 0)
    def _():
        sums_ref[...] = jnp.zeros_like(sums_ref)

    sums_ref[...] += row_of([cross, square], sums_ref.shape)


def first_combine(x, nu, parts, spins):
    size = x.shape[0]
    step = 128
    state = state_spec(spins, step, size)
    *y, sums = pl.pallas_call(
        functools.partial(first_combine_kernel, spins),
        grid=(size // step,),
        in_specs=[scalar_spec(), state] + part_specs(spins, step, size, len(parts)),
        out_specs=[state] * 3 + [scalar_spec()],
        out_shape=state_shapes(spins, size) + [SCALARS],
        compiler_params=params(),
    )(nu, x, *parts)
    return y, sums


def shift_kernel(nu_ref, parts_ref, out_ref):
    total = jnp.sum(parts_ref[...], axis=0)
    row = lax.broadcasted_iota(jnp.int32, out_ref.shape, 0)
    sigma = total[0:1, 0:1]
    tau = 1.0 / jnp.sqrt(total[0:1, 1:2])
    out_ref[...] = jnp.where(row == 0, sigma, jnp.where(row == 1, tau, nu_ref[...]))


def shift_rows(nu, parts):
    return pl.pallas_call(shift_kernel, out_shape=SCALARS, compiler_params=params())(nu, parts)


def combine_kernel(second, spins, scale_ref, w_ref, *refs):
    sigma, tau, nu = scale_ref[0:1, 0:1], scale_ref[1:2, 0:1], scale_ref[2:3, 0:1]
    if second:
        x_ref, refs = refs[0], refs[1:]
    part_refs, (out_ref, high_ref, low_ref) = refs[:-3], refs[-3:]
    size = part_refs[0].shape[2]
    for s, total in enumerate(add_parts(spins, part_refs)):
        cut = slice(s * size, (s + 1) * size)
        w = w_ref[:, cut]
        if second:
            inner = w - sigma * (nu * x_ref[:, cut])
            value = tau * tau * ((total - sigma * w) - sigma * inner)
        else:
            value = tau * (total - sigma * w)
        out_ref[:, cut] = value
        high_ref[:, cut], low_ref[:, cut] = split(value)


def combine(scales, w, x, parts, spins):
    size = w.shape[0]
    step = 128
    state = state_spec(spins, step, size)
    second = x is not None
    return pl.pallas_call(
        functools.partial(combine_kernel, second, spins),
        grid=(size // step,),
        in_specs=[scalar_spec()]
        + [state] * (2 if second else 1)
        + part_specs(spins, step, size, len(parts)),
        out_specs=[state] * 3,
        out_shape=state_shapes(spins, size),
        compiler_params=params(),
    )(scales, w, *([x] if second else []), *parts)


PAIRS = [(i, j) for j in range(5) for i in range(j + 1) if (i, j) != (4, 4)]


def gram_kernel(spins, place_ref, scale_ref, *refs):
    bases = [refs[k * spins : (k + 1) * spins] for k in range(4)]
    part_refs, out_ref = refs[4 * spins : -1], refs[-1]
    sigma, tau, nu = scale_ref[0:1, 0:1], scale_ref[1:2, 0:1], scale_ref[2:3, 0:1]
    sums = [jnp.zeros((8, 128), jnp.float32)] * len(PAIRS)
    chunk = 64
    size = part_refs[0].shape[1]
    for start in range(0, size, chunk):
        rows = slice(start, start + chunk)
        for s, total in enumerate(add_parts(spins, part_refs, rows)):
            x, y, w2, w3 = (bases[k][s][rows, :] for k in range(4))
            w = [nu * x, None, w2, w3, None]
            w[1] = tau * (y - sigma * w[0])
            w[4] = tau * (total - sigma * w[3])
            for p, (i, j) in enumerate(PAIRS):
                terms = (w[i] * w[j]).reshape(chunk // 8, 8, 128)
                sums[p] = sums[p] + jnp.sum(terms, axis=0)
    out_ref[...] = row_of([jnp.sum(value) for value in sums], out_ref.shape)


def gram_row(place, scales, states, parts, spins):
    size = states[0].shape[0]
    width = parts[0].shape[-1]
    per = size // width
    quarter = [
        pl.BlockSpec((size, width), functools.partial(lambda s, i, p: (0, s * per + p[0]), s))
        for s in range(spins)
    ]
    whole = [pl.BlockSpec((spins, size, width), lambda i, p: (0, 0, 0))]
    whole += [pl.BlockSpec((size, width), lambda i, p: (0, 0))] * (len(parts) - 1)
    flat = [state for state in states for s in range(spins)]
    return pl.pallas_call(
        functools.partial(gram_kernel, spins),
        grid_spec=pltpu.PrefetchScalarGridSpec(
            num_scalar_prefetch=1,
            grid=(1,),
            in_specs=[scalar_spec()] + quarter * 4 + whole,
            out_specs=scalar_spec(),
        ),
        out_shape=SCALARS,
        compiler_params=params(),
    )(place, scales, *flat, *parts)


def weights_kernel(step_size, scale_ref, sums_ref, out_ref):
    sigma, tau, nu = scale_ref[0:1], scale_ref[1:2], scale_ref[2:3]
    total = jnp.sum(sums_ref[...], axis=0)[0:1]
    gram = {}
    for p, (i, j) in enumerate(PAIRS):
        gram[(i, j)] = jnp.broadcast_to(total[:, p : p + 1], (1, 128))
    low = {}
    inverse = []
    for j in range(4):
        pivot = gram[(j, j)]
        for k in range(j):
            pivot = pivot - low[(j, k)] * low[(j, k)]
        low[(j, j)] = jnp.sqrt(pivot)
        inverse.append(1.0 / low[(j, j)])
        for i in range(j + 1, 5):
            value = gram[(j, i)]
            for k in range(j):
                value = value - low[(i, k)] * low[(j, k)]
            low[(i, j)] = value * inverse[j]
    stretch = 1.0 / tau
    beta = [low[(j + 1, j + 1)] * inverse[j] * stretch for j in range(3)]
    alpha = []
    for j in range(4):
        value = low[(j + 1, j)] * stretch
        if j > 0:
            value = value - low[(j, j - 1)] * beta[j - 1]
        alpha.append(sigma + value * inverse[j])
    factor = step_size / 16.0
    diag = [factor * a for a in alpha]
    off = [factor * b for b in beta]
    one = jnp.ones_like(sigma)
    zero = jnp.zeros_like(sigma)
    result = {(i, j): one if i == j else zero for i in range(4) for j in range(i, 4)}

    def entry(table, i, j):
        return table[(min(i, j), max(i, j))]

    for degree in range(8, 0, -1):
        fresh = {}
        for i in range(4):
            for j in range(i, 4):
                value = diag[i] * entry(result, i, j)
                if i > 0:
                    value = value + off[i - 1] * entry(result, i - 1, j)
                if i < 3:
                    value = value + off[i] * entry(result, i + 1, j)
                value = value * (1.0 / degree)
                fresh[(i, j)] = one + value if i == j else value
        result = fresh
    for squaring in range(4):
        fresh = {}
        for i in range(4):
            for j in range(i, 4):
                if squaring == 3 and i > 0:
                    continue
                value = entry(result, i, 0) * entry(result, 0, j)
                for k in range(1, 4):
                    value = value + entry(result, i, k) * entry(result, k, j)
                fresh[(i, j)] = value
        result = fresh
    column = [result[(0, j)] for j in range(4)]
    size = jnp.sqrt(sum(c * c for c in column))
    c = [None] * 4
    for i in range(3, -1, -1):
        value = column[i]
        for j in range(i + 1, 4):
            value = value - low[(j, i)] * c[j]
        c[i] = value * inverse[i]
    norm = low[(0, 0)] / nu
    c = [norm * v for v in c]
    rows = [(c[0] - c[1] * tau * sigma) * nu, c[1] * tau, c[2], c[3], 1.0 / (norm * size)]
    for p, value in enumerate(rows):
        out_ref[p : p + 1, :] = value
    for p in range(len(rows), 8):
        out_ref[p : p + 1, :] = zero


def basis_weights(scales, sums, step_size):
    return pl.pallas_call(
        functools.partial(weights_kernel, step_size),
        out_shape=SCALARS,
        compiler_params=params(),
    )(scales, sums)


def result_kernel(place_ref, weight_ref, *refs):
    value = weight_ref[0:1, 0:1] * refs[0][...]
    for k in range(1, 4):
        value = value + weight_ref[k : k + 1, 0:1] * refs[k][...]
    refs[4][...] = value


def weighted(place, weights, states, rows):
    size, columns = states[0].shape
    step = 128 if rows is None else rows
    if rows is None:
        spec = pl.BlockSpec((step, columns), lambda i, p: (i, 0))
    else:
        spec = pl.BlockSpec((step, columns), lambda i, p: (p[0], 0))
    return pl.pallas_call(
        result_kernel,
        grid_spec=pltpu.PrefetchScalarGridSpec(
            num_scalar_prefetch=1,
            grid=(size // step if rows is None else 1,),
            in_specs=[scalar_spec()] + [spec] * 4,
            out_specs=pl.BlockSpec((step, columns), lambda i, p: (i, 0)),
        ),
        out_shape=jax.ShapeDtypeStruct((size if rows is None else rows, columns), jnp.float32),
        compiler_params=params(),
    )(place, weights, *states)


def evolve(place, x, nu, apply_op, step_size, spins):
    parts, _ = apply_op(split_state(x), None, False)
    (y, *y_split), sums = first_combine(x, nu, parts, spins)
    parts, totals = apply_op(y_split, sums, False)
    scales = shift_rows(nu, totals)
    w2, *w2_split = combine(scales, y, x, parts, spins)
    parts, _ = apply_op(w2_split, None, False)
    w3, *w3_split = combine(scales, w2, None, parts, spins)
    parts, _ = apply_op(w3_split, None, True)
    states = [x, y, w2, w3]
    row = gram_row(place, scales, states, parts, spins)
    weights = basis_weights(scales, exchange(row, ("col", "sec")), step_size)
    return states, weights


def body(site_tensor, left_env, right_env, bond_env, sector_sizes):
    col_rows = site_tensor.shape[0]
    size = left_env.shape[2]
    sector = lax.axis_index("sec")
    last = lax.axis_size("sec") - 1
    place = lax.axis_index("col").reshape(1).astype(jnp.int32)

    left = left_env[0]
    site_block = site_tensor[:, 0]
    site_full = gather_col(site_block, 0)
    right_blocks = gather_col(right_env, 0)
    site_nu = inverse_norm(exchange(norm_row(site_block), ("col", "sec")))

    below_four = to_next(left[4])
    above_four = to_previous(left[4])
    below_sum = to_next(left[0] + left[1] + ANISOTROPY * left[4])
    above_sum = to_previous(left[0] - left[1] + ANISOTROPY * left[4])
    flags = jnp.stack([sector < last, sector > 0]).astype(jnp.int32)
    four, mix = left_parts(flags, left, below_sum, below_four, above_sum, above_four)
    stack, up, down = right_parts(right_blocks)
    bond = bond_parts(bond_env[0])

    def send_sums(sums, after):
        if sums is None:
            return None
        sums, _ = lax.optimization_barrier((sums, after))
        return exchange(sums, "sec")

    def apply_site(pair, sums, quarter):
        plain = ((), jnp.float32)
        d0, d1, u1, u2, zh, zl = product_call(
            site_send_kernel,
            place,
            [(True, pair[0]), (True, pair[1]), (False, four), (True, up), (True, down)],
            [four],
            [plain] * 4 + [((3,), BF16)] * 2,
            quarter,
            7 * UNIT,
        )
        d1, u1 = to_previous(d1), to_next(u1)
        d0, u2 = to_previous(d0), to_next(u2)
        totals = send_sums(sums, zh)
        (local,) = product_call(
            site_local_kernel,
            place,
            [(True, pair[0]), (True, pair[1]), (False, mix), (True, stack), (False, zh), (False, zl)],
            [mix],
            [((3,), jnp.float32)],
            quarter,
            13 * UNIT,
        )
        return [local, d0, d1, u1, u2], totals

    states, weights = evolve(place, site_full, site_nu, apply_site, -TIME_STEP, 3)
    evolved = weighted(place, weights, states, None)
    out_site = weighted(place, weights, states, col_rows)[:, None, :]
    gram = lax.dot_general(evolved, evolved, (((1,), (1,)), ((), ())), precision=HIGHEST)
    live = (jnp.arange(size) < sector_sizes[0]).astype(jnp.float32)
    gram = gram + (1.0 - live)[:, None] * jnp.eye(size, dtype=jnp.float32)
    factor = jnp.linalg.cholesky(gram[None])[0]
    bond_scale = math.sqrt(3.0 * size)
    start = factor * live[:, None] * live[None, :] / bond_scale
    bond_nu = jnp.broadcast_to(weights[4:5] * bond_scale, (8, 128))

    def apply_bond(pair, sums, quarter):
        plain = ((), jnp.float32)
        down_term, up_term = product_call(
            bond_send_kernel,
            place,
            [(True, pair[0]), (True, pair[1]), (False, bond), (True, up), (True, down)],
            [bond],
            [plain] * 2,
            quarter,
            4 * UNIT,
        )
        totals = send_sums(sums, up_term)
        down_term, up_term = to_previous(down_term), to_next(up_term)
        (local,) = product_call(
            bond_local_kernel,
            place,
            [(True, pair[0]), (True, pair[1]), (False, bond), (True, stack)],
            [bond],
            [((1,), jnp.float32)],
            quarter,
            6 * UNIT,
        )
        return [local, down_term, up_term], totals

    states, weights = evolve(place, start, bond_nu, apply_bond, TIME_STEP, 1)
    out_bond = weighted(place, weights, states, col_rows)[:, None, :]
    return (out_site, out_bond)


def solution(mesh):
    in_specs = (
        P("col", "sec", None),
        P("sec", None, None, None),
        P("sec", None, None, "col"),
        P("sec", None, None, None),
        P("sec"),
    )
    out_specs = (P("col", "sec", None), P("col", "sec", None))
    return jax.shard_map(body, mesh=mesh, in_specs=in_specs, out_specs=out_specs, check_vma=False)
```

```python
import functools
import math

import jax
import jax.numpy as jnp
from jax import lax
from jax.experimental import pallas as pl
from jax.experimental.pallas import tpu as pltpu
from jax.sharding import PartitionSpec as P

KRYLOV = 4
HIGHEST = lax.Precision.HIGHEST
ROOT_TWO = math.sqrt(2.0)
ANISOTROPY = 0.5
TIME_STEP = 0.1
VMEM_LIMIT = 56 * 1024 * 1024


def to_next(block):
    count = lax.axis_size("sec")
    return lax.ppermute(block, "sec", [(i, i + 1) for i in range(count - 1)])


def to_previous(block):
    count = lax.axis_size("sec")
    return lax.ppermute(block, "sec", [(i + 1, i) for i in range(count - 1)])


def gather_col(block, axis):
    return lax.all_gather(block, "col", axis=axis, tiled=True)


def params():
    return pltpu.CompilerParams(vmem_limit_bytes=VMEM_LIMIT)


def exchange(rows, axis):
    count = lax.axis_size(axis) if isinstance(axis, str) else lax.axis_size(axis[0]) * lax.axis_size(axis[1])
    sent = jnp.broadcast_to(rows[None], (count,) + rows.shape)
    return lax.all_to_all(sent, axis, 0, 0)


def row_of(values, shape):
    lane = lax.broadcasted_iota(jnp.int32, shape, 1)
    row = lax.broadcasted_iota(jnp.int32, shape, 0)
    out = jnp.zeros(shape, jnp.float32)
    for p, value in enumerate(values):
        out = jnp.where((lane == p) & (row == 0), value, out)
    return out


def add_parts(spins, part_refs, rows=slice(None)):
    local = part_refs[0]
    if spins == 1:
        return [local[0, rows, :] + part_refs[1][rows, :] + part_refs[2][rows, :]]
    down0, down1, up1, up2 = (ref[rows, :] for ref in part_refs[1:])
    return [local[0, rows, :] + up1, local[1, rows, :] + (up2 + down0), local[2, rows, :] + down1]


BF16 = jnp.bfloat16


def split(value):
    high = value.astype(BF16)
    return high, (value - high.astype(jnp.float32)).astype(BF16)


def product(left, right):
    def dot(a, b):
        return jnp.dot(a, b, preferred_element_type=jnp.float32)

    return dot(left[0], right[0]) + (dot(left[0], right[1]) + dot(left[1], right[0]))


SCALARS = jax.ShapeDtypeStruct((8, 128), jnp.float32)


def scalar_spec():
    return pl.BlockSpec((8, 128), lambda *i: (0, 0))


def norm_kernel(a_ref, out_ref):
    a = a_ref[...]
    out_ref[...] = row_of([jnp.sum(a * a)], out_ref.shape)


def norm_row(block):
    return pl.pallas_call(norm_kernel, out_shape=SCALARS, compiler_params=params())(block)


def inverse_norm_kernel(parts_ref, out_ref):
    total = jnp.sum(parts_ref[...], axis=0)
    out_ref[...] = jnp.broadcast_to(1.0 / jnp.sqrt(total[0:1, 0:1]), out_ref.shape)


def inverse_norm(parts):
    return pl.pallas_call(inverse_norm_kernel, out_shape=SCALARS, compiler_params=params())(parts)


def split_kernel(x_ref, high_ref, low_ref):
    high_ref[...], low_ref[...] = split(x_ref[...])


def split_state(x):
    rows, columns = x.shape
    step = 128
    spec = pl.BlockSpec((step, columns), lambda i: (i, 0))
    return pl.pallas_call(
        split_kernel,
        grid=(rows // step,),
        in_specs=[spec],
        out_specs=[spec] * 2,
        out_shape=[jax.ShapeDtypeStruct((rows, columns), BF16)] * 2,
        compiler_params=params(),
    )(x)


def right_kernel(block_ref, stack_ref, up_ref, down_ref):
    r0, r1, r2, r3, r4 = (block_ref[0, b] for b in range(5))
    for k, value in enumerate((r0, r4 + r1, r4, r4 - r1, r1)):
        stack_ref[k, 0], stack_ref[k, 1] = split(value)
    half = ROOT_TWO / 2
    up_ref[0], up_ref[1] = split(half * r2.T)
    down_ref[0], down_ref[1] = split(half * r3.T)


def right_parts(blocks):
    count, _, size, width = blocks.shape
    turned = pl.BlockSpec((2, width, size), lambda i: (0, i, 0))
    pair = jax.ShapeDtypeStruct((2, size, size), BF16)
    return pl.pallas_call(
        right_kernel,
        grid=(count,),
        in_specs=[pl.BlockSpec((1, 5, size, width), lambda i: (i, 0, 0, 0))],
        out_specs=[pl.BlockSpec((5, 2, size, width), lambda i: (0, 0, 0, i)), turned, turned],
        out_shape=[jax.ShapeDtypeStruct((5, 2, size, size), BF16), pair, pair],
        compiler_params=params(),
    )(blocks)


def left_kernel(flag_ref, left_ref, bsum_ref, bfour_ref, asum_ref, afour_ref, four_ref, mix_ref):
    has_above, has_below = flag_ref[0], flag_ref[1]
    for k, value in enumerate((bfour_ref[...], left_ref[4], afour_ref[...])):
        four_ref[k, 0], four_ref[k, 1] = split(value)
    raise_here = jnp.where(has_above > 0, ROOT_TWO * left_ref[2], 0.0)
    lower_here = jnp.where(has_below > 0, ROOT_TWO * left_ref[3], 0.0)
    mixes = (
        bsum_ref[...], lower_here, left_ref[0], lower_here.T, raise_here.T, asum_ref[...], raise_here
    )
    for k, value in enumerate(mixes):
        mix_ref[k, 0], mix_ref[k, 1] = split(value)


def left_parts(flags, left, below_sum, below_four, above_sum, above_four):
    size = left.shape[1]
    vmem = pl.BlockSpec(memory_space=pltpu.VMEM)
    return pl.pallas_call(
        left_kernel,
        in_specs=[pl.BlockSpec(memory_space=pltpu.SMEM)] + [vmem] * 5,
        out_specs=[vmem] * 2,
        out_shape=[
            jax.ShapeDtypeStruct((3, 2, size, size), BF16),
            jax.ShapeDtypeStruct((7, 2, size, size), BF16),
        ],
        compiler_params=params(),
    )(flags, left, below_sum, below_four, above_sum, above_four)


def bond_kernel(p_ref, out_ref):
    a = pl.program_id(0)
    scale = jnp.where((a == 2) | (a == 3), ROOT_TWO, 1.0).astype(jnp.float32)
    out_ref[0, 0], out_ref[0, 1] = split(scale * p_ref[0])


def bond_parts(bond):
    count, size, _ = bond.shape
    return pl.pallas_call(
        bond_kernel,
        grid=(count,),
        in_specs=[pl.BlockSpec((1, size, size), lambda i: (i, 0, 0))],
        out_specs=pl.BlockSpec((1, 2, size, size), lambda i: (i, 0, 0, 0)),
        out_shape=jax.ShapeDtypeStruct((count, 2, size, size), BF16),
        compiler_params=params(),
    )(bond)


def pair_of(ref, index):
    return ref[index, 0], ref[index, 1]


def columns_of(high_ref, low_ref, s):
    size = high_ref.shape[0]
    cut = slice(s * size, (s + 1) * size)
    return high_ref[:, cut], low_ref[:, cut]


def join(*blocks):
    return jnp.concatenate(blocks, axis=1)


def cut_columns(value, count):
    width = value.shape[1] // count
    return [value[:, i * width : (i + 1) * width] for i in range(count)]


class Fetch:
    def __init__(self, sems):
        self.sems = sems
        self.used = 0
        self.waiting = {}

    def start(self, name, source, target):
        copy = pltpu.make_async_copy(source, target, self.sems.at[self.used])
        self.used += 1
        copy.start()
        self.waiting[name] = copy

    def wait(self, *names):
        for name in names:
            if name in self.waiting:
                self.waiting.pop(name).wait()

    def wait_all(self):
        self.wait(*list(self.waiting))


def start_state(fetch, s, high, low, high_v, low_v):
    size = high_v.shape[1]
    cut = pl.ds(s * size, size)
    fetch.start(("xh", s), high.at[:, cut], high_v.at[s])
    fetch.start(("xl", s), low.at[:, cut], low_v.at[s])


def site_send_kernel(high, low, four, up, down, *refs):
    d0, d1, u1, u2, zh, zl = refs[:6]
    xh_v, xl_v, four_v, up_v, down_v, zh_v, zl_v, d_v, u_v, sems = refs[6:]
    fetch = Fetch(sems)
    for s in (1, 0, 2):
        start_state(fetch, s, high, low, xh_v, xl_v)
        fetch.start(("four", s), four.at[s], four_v.at[s])
        if s == 1:
            fetch.start("down", down, down_v)
            fetch.start("up", up, up_v)
    outs = Fetch(sems)
    outs.used = fetch.used
    for s in (1, 0, 2):
        fetch.wait(("xh", s), ("xl", s), ("four", s))
        z = product((xh_v[s], xl_v[s]), (four_v[s, 0], four_v[s, 1]))
        zh_v[s], zl_v[s] = split(z)
        outs.start(("zh", s), zh_v.at[s], zh.at[s])
        outs.start(("zl", s), zl_v.at[s], zl.at[s])
        pair = (zh_v[s], zl_v[s])
        if s < 2:
            fetch.wait("down")
            d_v[s] = product((down_v[0], down_v[1]), pair)
            outs.start(("d", s), d_v.at[s], (d0, d1)[s])
        if s > 0:
            fetch.wait("up")
            u_v[s - 1] = product((up_v[0], up_v[1]), pair)
            outs.start(("u", s), u_v.at[s - 1], (u1, u2)[s - 1])
    outs.wait_all()


TERMS = (((0, 0), (1, 1)), ((1, 2), (0, 3), (2, 4)), ((2, 5), (1, 6)))


def site_local_kernel(high, low, mix, stack, zh, zl, out, *refs):
    xh_v, xl_v, mix_v, stack_v, zh_v, zl_v, out_v, sems = refs
    fetch = Fetch(sems)
    seen = set()
    for s in range(3):
        for source, matrix in TERMS[s]:
            if source not in seen:
                seen.add(source)
                start_state(fetch, source, high, low, xh_v, xl_v)
            fetch.start(("mix", matrix), mix.at[matrix], mix_v.at[matrix])
        if s == 0:
            fetch.start(("stack", 0), stack.at[0], stack_v.at[0])
        fetch.start(("stack", 1 + s), stack.at[1 + s], stack_v.at[1 + s])
        fetch.start(("zh", s), zh.at[s], zh_v.at[s])
        fetch.start(("zl", s), zl.at[s], zl_v.at[s])
    outs = Fetch(sems)
    outs.used = fetch.used
    for s in range(3):
        total = None
        for source, matrix in TERMS[s]:
            fetch.wait(("xh", source), ("xl", source), ("mix", matrix))
            value = product((xh_v[source], xl_v[source]), (mix_v[matrix, 0], mix_v[matrix, 1]))
            total = value if total is None else total + value
        fetch.wait(("stack", 0), ("stack", 1 + s), ("zh", s), ("zl", s))
        y = product((stack_v[0, 0], stack_v[0, 1]), split(total))
        out_v[s] = y + product((stack_v[1 + s, 0], stack_v[1 + s, 1]), (zh_v[s], zl_v[s]))
        outs.start(("out", s), out_v.at[s], out.at[s])
    outs.wait_all()


def bond_send_kernel(high, low, bond, up, down, d_out, u_out, *refs):
    xh_v, xl_v, bond_v, up_v, down_v, d_v, u_v, sems = refs
    fetch = Fetch(sems)
    start_state(fetch, 0, high, low, xh_v, xl_v)
    fetch.start(("p", 3), bond.at[3], bond_v.at[1])
    fetch.start("down", down, down_v)
    fetch.start(("p", 2), bond.at[2], bond_v.at[0])
    fetch.start("up", up, up_v)
    outs = Fetch(sems)
    outs.used = fetch.used
    fetch.wait(("xh", 0), ("xl", 0), ("p", 3))
    x = (xh_v[0], xl_v[0])
    moved = split(product(x, (bond_v[1, 0], bond_v[1, 1])))
    fetch.wait("down")
    d_v[...] = product((down_v[0], down_v[1]), moved)
    outs.start("d", d_v, d_out)
    fetch.wait(("p", 2))
    moved = split(product(x, (bond_v[0, 0], bond_v[0, 1])))
    fetch.wait("up")
    u_v[...] = product((up_v[0], up_v[1]), moved)
    outs.start("u", u_v, u_out)
    outs.wait_all()


BOND_TERMS = ((0, 0), (4, 2), (1, 4))


def bond_local_kernel(high, low, bond, stack, out, *refs):
    xh_v, xl_v, bond_v, stack_v, out_v, sems = refs
    fetch = Fetch(sems)
    start_state(fetch, 0, high, low, xh_v, xl_v)
    for k, (a, matrix) in enumerate(BOND_TERMS):
        fetch.start(("p", k), bond.at[a], bond_v.at[k])
        fetch.start(("r", k), stack.at[matrix], stack_v.at[k])
    total = None
    for k in range(3):
        fetch.wait(("xh", 0), ("xl", 0), ("p", k))
        moved = split(product((xh_v[0], xl_v[0]), (bond_v[k, 0], bond_v[k, 1])))
        fetch.wait(("r", k))
        value = product((stack_v[k, 0], stack_v[k, 1]), moved)
        total = value if total is None else total + value
    out_v[...] = total
    outs = Fetch(sems)
    outs.used = fetch.used
    outs.start("out", out_v, out.at[0])
    outs.wait_all()


def site_send_quarter(place_ref, high, low, four_ref, up_ref, down_ref, d0, d1, u1, u2, zh, zl):
    z = [product(columns_of(high, low, s), pair_of(four_ref, s)) for s in range(3)]
    for s in range(3):
        zh[s], zl[s] = split(z[s])
    d0[...], d1[...] = cut_columns(product((down_ref[0], down_ref[1]), split(join(z[0], z[1]))), 2)
    u1[...], u2[...] = cut_columns(product((up_ref[0], up_ref[1]), split(join(z[1], z[2]))), 2)


def site_local_quarter(place_ref, high, low, mix_ref, stack_ref, zh, zl, out_ref):
    def merged(s, *matrices):
        right = (join(*[mix_ref[m, part] for m in matrices]) for part in range(2))
        return cut_columns(product(columns_of(high, low, s), tuple(right)), len(matrices))

    p0, p1 = merged(0, 0, 3)
    more0, more1, p2 = merged(1, 1, 2, 6)
    last2, last1 = merged(2, 5, 4)
    mixed = split(join(p0 + more0, p1 + more1 + last1, p2 + last2))
    y = cut_columns(product(pair_of(stack_ref, 0), mixed), 3)
    for s in range(3):
        out_ref[s] = y[s] + product(pair_of(stack_ref, 1 + s), (zh[s], zl[s]))


def bond_send_quarter(place_ref, high, low, p_ref, up_ref, down_ref, d_ref, u_ref):
    right = (join(p_ref[3, part], p_ref[2, part]) for part in range(2))
    down, up = cut_columns(product((high[...], low[...]), tuple(right)), 2)
    d_ref[...] = product((down_ref[0], down_ref[1]), split(down))
    u_ref[...] = product((up_ref[0], up_ref[1]), split(up))


def bond_local_quarter(place_ref, high, low, p_ref, stack_ref, out_ref):
    right = (join(*[p_ref[a, part] for a, _ in BOND_TERMS]) for part in range(2))
    moved = cut_columns(product((high[...], low[...]), tuple(right)), 3)
    total = None
    for value, (_, matrix) in zip(moved, BOND_TERMS):
        value = product(pair_of(stack_ref, matrix), split(value))
        total = value if total is None else total + value
    out_ref[0] = total


UNIT = 6 * 512**3


def quarter_call(kernel, place, operands, outs, products):
    size = operands[0][1].shape[0]
    width = size // 4

    def spec(is_whole, array):
        lead = (0,) * (array.ndim - 1)
        if is_whole:
            return pl.BlockSpec(array.shape, lambda i, p: lead + (0,))
        return pl.BlockSpec(array.shape[:-1] + (width,), lambda i, p: lead + (p[0],))

    shapes = [jax.ShapeDtypeStruct(shape + (size, width), dtype) for shape, dtype in outs]
    return pl.pallas_call(
        kernel,
        grid_spec=pltpu.PrefetchScalarGridSpec(
            num_scalar_prefetch=1,
            grid=(1,),
            in_specs=[spec(*operand) for operand in operands],
            out_specs=[spec(True, shape) for shape in shapes],
        ),
        out_shape=shapes,
        compiler_params=params(),
        cost_estimate=pl.CostEstimate(
            flops=products * UNIT // 4, bytes_accessed=12 * 2**20, transcendentals=0
        ),
    )(place, *[array for _, array in operands])


def full_call(kernel, operands, outs, scratch, copies, products):
    anywhere = pl.BlockSpec(memory_space=pl.ANY)
    return pl.pallas_call(
        kernel,
        in_specs=[anywhere] * len(operands),
        out_specs=[anywhere] * len(outs),
        out_shape=[jax.ShapeDtypeStruct(shape, dtype) for shape, dtype in outs],
        scratch_shapes=[pltpu.VMEM(shape, dtype) for shape, dtype in scratch]
        + [pltpu.SemaphoreType.DMA((copies,))],
        compiler_params=params(),
        cost_estimate=pl.CostEstimate(
            flops=products * UNIT, bytes_accessed=16 * 2**20, transcendentals=0
        ),
    )(*operands)


def state_spec(spins, step, size):
    return pl.BlockSpec((step, spins * size), lambda i: (i, 0))


def part_specs(spins, step, size, count):
    row = pl.BlockSpec((step, size), lambda i: (i, 0))
    return [pl.BlockSpec((spins, step, size), lambda i: (0, i, 0))] + [row] * (count - 1)


def state_shapes(spins, size):
    full = (size, spins * size)
    return [jax.ShapeDtypeStruct(full, t) for t in (jnp.float32, BF16, BF16)]


def first_combine_kernel(spins, scale_ref, x_ref, *refs):
    part_refs, (y_ref, high_ref, low_ref, sums_ref) = refs[:-4], refs[-4:]
    nu = scale_ref[2:3, 0:1]
    size = part_refs[0].shape[2]
    cross = jnp.float32(0.0)
    square = jnp.float32(0.0)
    for s, total in enumerate(add_parts(spins, part_refs)):
        cut = slice(s * size, (s + 1) * size)
        y = total * nu
        y_ref[:, cut] = y
        high_ref[:, cut], low_ref[:, cut] = split(y)
        cross += jnp.sum(x_ref[:, cut] * nu * y)
        square += jnp.sum(y * y)

    @pl.when(pl.program_id(0) == 0)
    def _():
        sums_ref[...] = jnp.zeros_like(sums_ref)

    sums_ref[...] += row_of([cross, square], sums_ref.shape)


def first_combine(x, nu, parts, spins):
    size = x.shape[0]
    step = 128
    state = state_spec(spins, step, size)
    *y, sums = pl.pallas_call(
        functools.partial(first_combine_kernel, spins),
        grid=(size // step,),
        in_specs=[scalar_spec(), state] + part_specs(spins, step, size, len(parts)),
        out_specs=[state] * 3 + [scalar_spec()],
        out_shape=state_shapes(spins, size) + [SCALARS],
        compiler_params=params(),
    )(nu, x, *parts)
    return y, sums


def shift_kernel(nu_ref, parts_ref, out_ref):
    total = jnp.sum(parts_ref[...], axis=0)
    row = lax.broadcasted_iota(jnp.int32, out_ref.shape, 0)
    sigma = total[0:1, 0:1]
    tau = 1.0 / jnp.sqrt(total[0:1, 1:2])
    out_ref[...] = jnp.where(row == 0, sigma, jnp.where(row == 1, tau, nu_ref[...]))


def shift_rows(nu, parts):
    return pl.pallas_call(shift_kernel, out_shape=SCALARS, compiler_params=params())(nu, parts)


def combine_kernel(second, spins, scale_ref, w_ref, *refs):
    sigma, tau, nu = scale_ref[0:1, 0:1], scale_ref[1:2, 0:1], scale_ref[2:3, 0:1]
    if second:
        x_ref, refs = refs[0], refs[1:]
    part_refs, (out_ref, high_ref, low_ref) = refs[:-3], refs[-3:]
    size = part_refs[0].shape[2]
    for s, total in enumerate(add_parts(spins, part_refs)):
        cut = slice(s * size, (s + 1) * size)
        w = w_ref[:, cut]
        if second:
            inner = w - sigma * (nu * x_ref[:, cut])
            value = tau * tau * ((total - sigma * w) - sigma * inner)
        else:
            value = tau * (total - sigma * w)
        out_ref[:, cut] = value
        high_ref[:, cut], low_ref[:, cut] = split(value)


def combine(scales, w, x, parts, spins):
    size = w.shape[0]
    step = 128
    state = state_spec(spins, step, size)
    second = x is not None
    return pl.pallas_call(
        functools.partial(combine_kernel, second, spins),
        grid=(size // step,),
        in_specs=[scalar_spec()]
        + [state] * (2 if second else 1)
        + part_specs(spins, step, size, len(parts)),
        out_specs=[state] * 3,
        out_shape=state_shapes(spins, size),
        compiler_params=params(),
    )(scales, w, *([x] if second else []), *parts)


PAIRS = [(i, j) for j in range(5) for i in range(j + 1) if (i, j) != (4, 4)]


def gram_kernel(spins, place_ref, scale_ref, *refs):
    bases = [refs[k * spins : (k + 1) * spins] for k in range(4)]
    part_refs, out_ref = refs[4 * spins : -1], refs[-1]
    sigma, tau, nu = scale_ref[0:1, 0:1], scale_ref[1:2, 0:1], scale_ref[2:3, 0:1]
    sums = [jnp.zeros((8, 128), jnp.float32)] * len(PAIRS)
    chunk = 64
    size = part_refs[0].shape[1]
    for start in range(0, size, chunk):
        rows = slice(start, start + chunk)
        for s, total in enumerate(add_parts(spins, part_refs, rows)):
            x, y, w2, w3 = (bases[k][s][rows, :] for k in range(4))
            w = [nu * x, None, w2, w3, None]
            w[1] = tau * (y - sigma * w[0])
            w[4] = tau * (total - sigma * w[3])
            for p, (i, j) in enumerate(PAIRS):
                terms = (w[i] * w[j]).reshape(chunk // 8, 8, 128)
                sums[p] = sums[p] + jnp.sum(terms, axis=0)
    out_ref[...] = row_of([jnp.sum(value) for value in sums], out_ref.shape)


def gram_row(place, scales, states, parts, spins):
    size = states[0].shape[0]
    width = parts[0].shape[-1]
    per = size // width
    quarter = [
        pl.BlockSpec((size, width), functools.partial(lambda s, i, p: (0, s * per + p[0]), s))
        for s in range(spins)
    ]
    whole = [pl.BlockSpec((spins, size, width), lambda i, p: (0, 0, 0))]
    whole += [pl.BlockSpec((size, width), lambda i, p: (0, 0))] * (len(parts) - 1)
    flat = [state for state in states for s in range(spins)]
    return pl.pallas_call(
        functools.partial(gram_kernel, spins),
        grid_spec=pltpu.PrefetchScalarGridSpec(
            num_scalar_prefetch=1,
            grid=(1,),
            in_specs=[scalar_spec()] + quarter * 4 + whole,
            out_specs=scalar_spec(),
        ),
        out_shape=SCALARS,
        compiler_params=params(),
    )(place, scales, *flat, *parts)


def weights_kernel(step_size, scale_ref, sums_ref, out_ref):
    sigma, tau, nu = scale_ref[0:1], scale_ref[1:2], scale_ref[2:3]
    total = jnp.sum(sums_ref[...], axis=0)[0:1]
    gram = {}
    for p, (i, j) in enumerate(PAIRS):
        gram[(i, j)] = jnp.broadcast_to(total[:, p : p + 1], (1, 128))
    low = {}
    inverse = []
    for j in range(4):
        pivot = gram[(j, j)]
        for k in range(j):
            pivot = pivot - low[(j, k)] * low[(j, k)]
        low[(j, j)] = jnp.sqrt(pivot)
        inverse.append(1.0 / low[(j, j)])
        for i in range(j + 1, 5):
            value = gram[(j, i)]
            for k in range(j):
                value = value - low[(i, k)] * low[(j, k)]
            low[(i, j)] = value * inverse[j]
    stretch = 1.0 / tau
    beta = [low[(j + 1, j + 1)] * inverse[j] * stretch for j in range(3)]
    alpha = []
    for j in range(4):
        value = low[(j + 1, j)] * stretch
        if j > 0:
            value = value - low[(j, j - 1)] * beta[j - 1]
        alpha.append(sigma + value * inverse[j])
    factor = step_size / 16.0
    diag = [factor * a for a in alpha]
    off = [factor * b for b in beta]
    one = jnp.ones_like(sigma)
    zero = jnp.zeros_like(sigma)
    result = {(i, j): one if i == j else zero for i in range(4) for j in range(i, 4)}

    def entry(table, i, j):
        return table[(min(i, j), max(i, j))]

    for degree in range(8, 0, -1):
        fresh = {}
        for i in range(4):
            for j in range(i, 4):
                value = diag[i] * entry(result, i, j)
                if i > 0:
                    value = value + off[i - 1] * entry(result, i - 1, j)
                if i < 3:
                    value = value + off[i] * entry(result, i + 1, j)
                value = value * (1.0 / degree)
                fresh[(i, j)] = one + value if i == j else value
        result = fresh
    for squaring in range(4):
        fresh = {}
        for i in range(4):
            for j in range(i, 4):
                if squaring == 3 and i > 0:
                    continue
                value = entry(result, i, 0) * entry(result, 0, j)
                for k in range(1, 4):
                    value = value + entry(result, i, k) * entry(result, k, j)
                fresh[(i, j)] = value
        result = fresh
    column = [result[(0, j)] for j in range(4)]
    size = jnp.sqrt(sum(c * c for c in column))
    c = [None] * 4
    for i in range(3, -1, -1):
        value = column[i]
        for j in range(i + 1, 4):
            value = value - low[(j, i)] * c[j]
        c[i] = value * inverse[i]
    norm = low[(0, 0)] / nu
    c = [norm * v for v in c]
    rows = [(c[0] - c[1] * tau * sigma) * nu, c[1] * tau, c[2], c[3], 1.0 / (norm * size)]
    for p, value in enumerate(rows):
        out_ref[p : p + 1, :] = value
    for p in range(len(rows), 8):
        out_ref[p : p + 1, :] = zero


def basis_weights(scales, sums, step_size):
    return pl.pallas_call(
        functools.partial(weights_kernel, step_size),
        out_shape=SCALARS,
        compiler_params=params(),
    )(scales, sums)


def result_kernel(place_ref, weight_ref, *refs):
    value = weight_ref[0:1, 0:1] * refs[0][...]
    for k in range(1, 4):
        value = value + weight_ref[k : k + 1, 0:1] * refs[k][...]
    refs[4][...] = value


def weighted(place, weights, states, rows):
    size, columns = states[0].shape
    step = 128 if rows is None else rows
    if rows is None:
        spec = pl.BlockSpec((step, columns), lambda i, p: (i, 0))
    else:
        spec = pl.BlockSpec((step, columns), lambda i, p: (p[0], 0))
    return pl.pallas_call(
        result_kernel,
        grid_spec=pltpu.PrefetchScalarGridSpec(
            num_scalar_prefetch=1,
            grid=(size // step if rows is None else 1,),
            in_specs=[scalar_spec()] + [spec] * 4,
            out_specs=pl.BlockSpec((step, columns), lambda i, p: (i, 0)),
        ),
        out_shape=jax.ShapeDtypeStruct((size if rows is None else rows, columns), jnp.float32),
        compiler_params=params(),
    )(place, weights, *states)


def evolve(place, x, nu, apply_op, step_size, spins):
    parts, _ = apply_op(split_state(x), None, False)
    (y, *y_split), sums = first_combine(x, nu, parts, spins)
    parts, totals = apply_op(y_split, sums, False)
    scales = shift_rows(nu, totals)
    w2, *w2_split = combine(scales, y, x, parts, spins)
    parts, _ = apply_op(w2_split, None, False)
    w3, *w3_split = combine(scales, w2, None, parts, spins)
    parts, _ = apply_op(w3_split, None, True)
    states = [x, y, w2, w3]
    row = gram_row(place, scales, states, parts, spins)
    weights = basis_weights(scales, exchange(row, ("col", "sec")), step_size)
    return states, weights


def body(site_tensor, left_env, right_env, bond_env, sector_sizes):
    col_rows = site_tensor.shape[0]
    size = left_env.shape[2]
    sector = lax.axis_index("sec")
    last = lax.axis_size("sec") - 1
    place = lax.axis_index("col").reshape(1).astype(jnp.int32)

    left = left_env[0]
    site_block = site_tensor[:, 0]
    site_full = gather_col(site_block, 0)
    right_blocks = gather_col(right_env, 0)
    site_nu = inverse_norm(exchange(norm_row(site_block), ("col", "sec")))

    below_four = to_next(left[4])
    above_four = to_previous(left[4])
    below_sum = to_next(left[0] + left[1] + ANISOTROPY * left[4])
    above_sum = to_previous(left[0] - left[1] + ANISOTROPY * left[4])
    flags = jnp.stack([sector < last, sector > 0]).astype(jnp.int32)
    four, mix = left_parts(flags, left, below_sum, below_four, above_sum, above_four)
    stack, up, down = right_parts(right_blocks)
    bond = bond_parts(bond_env[0])

    def send_sums(sums, after):
        if sums is None:
            return None
        sums, _ = lax.optimization_barrier((sums, after))
        return exchange(sums, "sec")

    matrix = (size, size)
    thirds = ((3,) + matrix, BF16)
    pairs = ((2,) + matrix, BF16)
    f32 = jnp.float32

    def apply_site(pair, sums, quarter):
        if quarter:
            d0, d1, u1, u2, zh, zl = quarter_call(
                site_send_quarter,
                place,
                [(True, pair[0]), (True, pair[1]), (False, four), (True, up), (True, down)],
                [((), f32)] * 4 + [((3,), BF16)] * 2,
                7,
            )
        else:
            d0, d1, u1, u2, zh, zl = full_call(
                site_send_kernel,
                [pair[0], pair[1], four, up, down],
                [(matrix, f32)] * 4 + [thirds] * 2,
                [thirds, thirds, ((3, 2) + matrix, BF16), pairs, pairs, thirds, thirds]
                + [((2,) + matrix, f32)] * 2,
                24,
                7,
            )
        d1, u1 = to_previous(d1), to_next(u1)
        d0, u2 = to_previous(d0), to_next(u2)
        totals = send_sums(sums, zh)
        if quarter:
            (local,) = quarter_call(
                site_local_quarter,
                place,
                [(True, pair[0]), (True, pair[1]), (False, mix), (True, stack), (True, zh), (True, zl)],
                [((3,), f32)],
                13,
            )
        else:
            (local,) = full_call(
                site_local_kernel,
                [pair[0], pair[1], mix, stack, zh, zl],
                [((3,) + matrix, f32)],
                [thirds, thirds, ((7, 2) + matrix, BF16), ((4, 2) + matrix, BF16), thirds, thirds]
                + [((3,) + matrix, f32)],
                32,
                13,
            )
        return [local, d0, d1, u1, u2], totals

    states, weights = evolve(place, site_full, site_nu, apply_site, -TIME_STEP, 3)
    evolved = weighted(place, weights, states, None)
    out_site = weighted(place, weights, states, col_rows)[:, None, :]
    gram = lax.dot_general(evolved, evolved, (((1,), (1,)), ((), ())), precision=HIGHEST)
    live = (jnp.arange(size) < sector_sizes[0]).astype(jnp.float32)
    gram = gram + (1.0 - live)[:, None] * jnp.eye(size, dtype=jnp.float32)
    factor = jnp.linalg.cholesky(gram[None])[0]
    bond_scale = math.sqrt(3.0 * size)
    start = factor * live[:, None] * live[None, :] / bond_scale
    bond_nu = jnp.broadcast_to(weights[4:5] * bond_scale, (8, 128))

    single = ((1,) + matrix, BF16)

    def apply_bond(pair, sums, quarter):
        if quarter:
            down_term, up_term = quarter_call(
                bond_send_quarter,
                place,
                [(True, pair[0]), (True, pair[1]), (False, bond), (True, up), (True, down)],
                [((), f32)] * 2,
                4,
            )
        else:
            down_term, up_term = full_call(
                bond_send_kernel,
                [pair[0], pair[1], bond, up, down],
                [(matrix, f32)] * 2,
                [single, single, ((2, 2) + matrix, BF16), pairs, pairs] + [(matrix, f32)] * 2,
                8,
                4,
            )
        totals = send_sums(sums, up_term)
        down_term, up_term = to_previous(down_term), to_next(up_term)
        if quarter:
            (local,) = quarter_call(
                bond_local_quarter,
                place,
                [(True, pair[0]), (True, pair[1]), (False, bond), (True, stack)],
                [((1,), f32)],
                6,
            )
        else:
            (local,) = full_call(
                bond_local_kernel,
                [pair[0], pair[1], bond, stack],
                [((1,) + matrix, f32)],
                [single, single, ((3, 2) + matrix, BF16), ((3, 2) + matrix, BF16), (matrix, f32)],
                9,
                6,
            )
        return [local, down_term, up_term], totals

    states, weights = evolve(place, start, bond_nu, apply_bond, TIME_STEP, 1)
    out_bond = weighted(place, weights, states, col_rows)[:, None, :]
    return (out_site, out_bond)


def solution(mesh):
    in_specs = (
        P("col", "sec", None),
        P("sec", None, None, None),
        P("sec", None, None, "col"),
        P("sec", None, None, None),
        P("sec"),
    )
    out_specs = (P("col", "sec", None), P("col", "sec", None))
    return jax.shard_map(body, mesh=mesh, in_specs=in_specs, out_specs=out_specs, check_vma=False)
```

```python
import functools
import math

import jax
import jax.numpy as jnp
from jax import lax
from jax.experimental import pallas as pl
from jax.experimental.pallas import tpu as pltpu
from jax.sharding import PartitionSpec as P

KRYLOV = 4
HIGHEST = lax.Precision.HIGHEST
ROOT_TWO = math.sqrt(2.0)
ANISOTROPY = 0.5
TIME_STEP = 0.1
VMEM_LIMIT = 56 * 1024 * 1024


def to_next(block):
    count = lax.axis_size("sec")
    return lax.ppermute(block, "sec", [(i, i + 1) for i in range(count - 1)])


def to_previous(block):
    count = lax.axis_size("sec")
    return lax.ppermute(block, "sec", [(i + 1, i) for i in range(count - 1)])


def gather_col(block, axis):
    return lax.all_gather(block, "col", axis=axis, tiled=True)


def params():
    return pltpu.CompilerParams(vmem_limit_bytes=VMEM_LIMIT)


def exchange(rows, axis):
    count = lax.axis_size(axis) if isinstance(axis, str) else lax.axis_size(axis[0]) * lax.axis_size(axis[1])
    sent = jnp.broadcast_to(rows[None], (count,) + rows.shape)
    return lax.all_to_all(sent, axis, 0, 0)


def row_of(values, shape):
    lane = lax.broadcasted_iota(jnp.int32, shape, 1)
    row = lax.broadcasted_iota(jnp.int32, shape, 0)
    out = jnp.zeros(shape, jnp.float32)
    for p, value in enumerate(values):
        out = jnp.where((lane == p) & (row == 0), value, out)
    return out


def add_parts(spins, part_refs, rows=slice(None)):
    local = part_refs[0]
    if spins == 1:
        return [local[0, rows, :] + part_refs[1][0, rows, :] + part_refs[2][0, rows, :]]
    down0, down1 = (part_refs[1][k, rows, :] for k in range(2))
    up1, up2 = (part_refs[2][k, rows, :] for k in range(2))
    return [local[0, rows, :] + up1, local[1, rows, :] + (up2 + down0), local[2, rows, :] + down1]


BF16 = jnp.bfloat16


def split(value):
    high = value.astype(BF16)
    return high, (value - high.astype(jnp.float32)).astype(BF16)


def product(left, right):
    def dot(a, b):
        return jnp.dot(a, b, preferred_element_type=jnp.float32)

    return dot(left[0], right[0]) + (dot(left[0], right[1]) + dot(left[1], right[0]))


SCALARS = jax.ShapeDtypeStruct((8, 128), jnp.float32)


def scalar_spec():
    return pl.BlockSpec((8, 128), lambda *i: (0, 0))


def norm_kernel(a_ref, out_ref):
    a = a_ref[...]
    out_ref[...] = row_of([jnp.sum(a * a)], out_ref.shape)


def norm_row(block):
    return pl.pallas_call(norm_kernel, out_shape=SCALARS, compiler_params=params())(block)


def inverse_norm_kernel(parts_ref, out_ref):
    total = jnp.sum(parts_ref[...], axis=0)
    out_ref[...] = jnp.broadcast_to(1.0 / jnp.sqrt(total[0:1, 0:1]), out_ref.shape)


def inverse_norm(parts):
    return pl.pallas_call(inverse_norm_kernel, out_shape=SCALARS, compiler_params=params())(parts)


def split_kernel(x_ref, high_ref, low_ref):
    high_ref[...], low_ref[...] = split(x_ref[...])


def split_state(x):
    rows, columns = x.shape
    step = 128
    spec = pl.BlockSpec((step, columns), lambda i: (i, 0))
    return pl.pallas_call(
        split_kernel,
        grid=(rows // step,),
        in_specs=[spec],
        out_specs=[spec] * 2,
        out_shape=[jax.ShapeDtypeStruct((rows, columns), BF16)] * 2,
        compiler_params=params(),
    )(x)


def right_kernel(block_ref, stack_ref, up_ref, down_ref):
    r0, r1, r2, r3, r4 = (block_ref[0, b] for b in range(5))
    for k, value in enumerate((r0, r4 + r1, r4, r4 - r1, r1)):
        stack_ref[k, 0], stack_ref[k, 1] = split(value)
    half = ROOT_TWO / 2
    up_ref[0], up_ref[1] = split(half * r2.T)
    down_ref[0], down_ref[1] = split(half * r3.T)


def right_parts(blocks):
    count, _, size, width = blocks.shape
    turned = pl.BlockSpec((2, width, size), lambda i: (0, i, 0))
    pair = jax.ShapeDtypeStruct((2, size, size), BF16)
    return pl.pallas_call(
        right_kernel,
        grid=(count,),
        in_specs=[pl.BlockSpec((1, 5, size, width), lambda i: (i, 0, 0, 0))],
        out_specs=[pl.BlockSpec((5, 2, size, width), lambda i: (0, 0, 0, i)), turned, turned],
        out_shape=[jax.ShapeDtypeStruct((5, 2, size, size), BF16), pair, pair],
        compiler_params=params(),
    )(blocks)


def left_kernel(flag_ref, left_ref, bsum_ref, bfour_ref, asum_ref, afour_ref, four_ref, mix_ref):
    has_above, has_below = flag_ref[0], flag_ref[1]
    for k, value in enumerate((bfour_ref[...], left_ref[4], afour_ref[...])):
        four_ref[k, 0], four_ref[k, 1] = split(value)
    raise_here = jnp.where(has_above > 0, ROOT_TWO * left_ref[2], 0.0)
    lower_here = jnp.where(has_below > 0, ROOT_TWO * left_ref[3], 0.0)
    mixes = (
        bsum_ref[...], lower_here, left_ref[0], lower_here.T, raise_here.T, asum_ref[...], raise_here
    )
    for k, value in enumerate(mixes):
        mix_ref[k, 0], mix_ref[k, 1] = split(value)


def left_parts(flags, left, below_sum, below_four, above_sum, above_four):
    size = left.shape[1]
    vmem = pl.BlockSpec(memory_space=pltpu.VMEM)
    return pl.pallas_call(
        left_kernel,
        in_specs=[pl.BlockSpec(memory_space=pltpu.SMEM)] + [vmem] * 5,
        out_specs=[vmem] * 2,
        out_shape=[
            jax.ShapeDtypeStruct((3, 2, size, size), BF16),
            jax.ShapeDtypeStruct((7, 2, size, size), BF16),
        ],
        compiler_params=params(),
    )(flags, left, below_sum, below_four, above_sum, above_four)


def bond_kernel(p_ref, out_ref):
    a = pl.program_id(0)
    scale = jnp.where((a == 2) | (a == 3), ROOT_TWO, 1.0).astype(jnp.float32)
    out_ref[0, 0], out_ref[0, 1] = split(scale * p_ref[0])


def bond_parts(bond):
    count, size, _ = bond.shape
    return pl.pallas_call(
        bond_kernel,
        grid=(count,),
        in_specs=[pl.BlockSpec((1, size, size), lambda i: (i, 0, 0))],
        out_specs=pl.BlockSpec((1, 2, size, size), lambda i: (i, 0, 0, 0)),
        out_shape=jax.ShapeDtypeStruct((count, 2, size, size), BF16),
        compiler_params=params(),
    )(bond)


def pair_of(ref, index):
    return ref[index, 0], ref[index, 1]


def columns_of(high_ref, low_ref, s):
    size = high_ref.shape[0]
    cut = slice(s * size, (s + 1) * size)
    return high_ref[:, cut], low_ref[:, cut]


def join(*blocks):
    return jnp.concatenate(blocks, axis=1)


def cut_columns(value, count):
    width = value.shape[1] // count
    return [value[:, i * width : (i + 1) * width] for i in range(count)]


class Fetch:
    def __init__(self, sems):
        self.sems = sems
        self.used = 0
        self.waiting = {}

    def start(self, name, source, target):
        copy = pltpu.make_async_copy(source, target, self.sems.at[self.used])
        self.used += 1
        copy.start()
        self.waiting[name] = copy

    def wait(self, *names):
        for name in names:
            if name in self.waiting:
                self.waiting.pop(name).wait()

    def wait_all(self):
        self.wait(*list(self.waiting))


def start_state(fetch, s, high, low, high_v, low_v):
    size = high_v.shape[1]
    cut = pl.ds(s * size, size)
    fetch.start(("xh", s), high.at[:, cut], high_v.at[s])
    fetch.start(("xl", s), low.at[:, cut], low_v.at[s])


def site_send_kernel(high, low, four, up, down, *refs):
    d_out, u_out, zh, zl = refs[:4]
    xh_v, xl_v, four_v, up_v, down_v, zh_v, zl_v, d_v, u_v, sems = refs[4:]
    fetch = Fetch(sems)
    for s in (1, 0, 2):
        start_state(fetch, s, high, low, xh_v, xl_v)
        fetch.start(("four", s), four.at[s], four_v.at[s])
        if s == 1:
            fetch.start("down", down, down_v)
            fetch.start("up", up, up_v)
    outs = Fetch(sems)
    outs.used = fetch.used
    for s in (1, 0, 2):
        fetch.wait(("xh", s), ("xl", s), ("four", s))
        z = product((xh_v[s], xl_v[s]), (four_v[s, 0], four_v[s, 1]))
        zh_v[s], zl_v[s] = split(z)
        outs.start(("zh", s), zh_v.at[s], zh.at[s])
        outs.start(("zl", s), zl_v.at[s], zl.at[s])
        pair = (zh_v[s], zl_v[s])
        if s < 2:
            fetch.wait("down")
            d_v[s] = product((down_v[0], down_v[1]), pair)
            outs.start(("d", s), d_v.at[s], d_out.at[s])
        if s > 0:
            fetch.wait("up")
            u_v[s - 1] = product((up_v[0], up_v[1]), pair)
            outs.start(("u", s), u_v.at[s - 1], u_out.at[s - 1])
    outs.wait_all()


TERMS = (((0, 0), (1, 1)), ((1, 2), (0, 3), (2, 4)), ((2, 5), (1, 6)))


def site_local_kernel(high, low, mix, stack, zh, zl, out, *refs):
    xh_v, xl_v, mix_v, stack_v, zh_v, zl_v, out_v, sems = refs
    fetch = Fetch(sems)
    seen = set()
    for s in range(3):
        for source, matrix in TERMS[s]:
            if source not in seen:
                seen.add(source)
                start_state(fetch, source, high, low, xh_v, xl_v)
            fetch.start(("mix", matrix), mix.at[matrix], mix_v.at[matrix])
        if s == 0:
            fetch.start(("stack", 0), stack.at[0], stack_v.at[0])
        fetch.start(("stack", 1 + s), stack.at[1 + s], stack_v.at[1 + s])
        fetch.start(("zh", s), zh.at[s], zh_v.at[s])
        fetch.start(("zl", s), zl.at[s], zl_v.at[s])
    outs = Fetch(sems)
    outs.used = fetch.used
    for s in range(3):
        total = None
        for source, matrix in TERMS[s]:
            fetch.wait(("xh", source), ("xl", source), ("mix", matrix))
            value = product((xh_v[source], xl_v[source]), (mix_v[matrix, 0], mix_v[matrix, 1]))
            total = value if total is None else total + value
        fetch.wait(("stack", 0), ("stack", 1 + s), ("zh", s), ("zl", s))
        y = product((stack_v[0, 0], stack_v[0, 1]), split(total))
        out_v[s] = y + product((stack_v[1 + s, 0], stack_v[1 + s, 1]), (zh_v[s], zl_v[s]))
        outs.start(("out", s), out_v.at[s], out.at[s])
    outs.wait_all()


def bond_send_kernel(high, low, bond, up, down, d_out, u_out, *refs):
    xh_v, xl_v, bond_v, up_v, down_v, d_v, u_v, sems = refs
    fetch = Fetch(sems)
    start_state(fetch, 0, high, low, xh_v, xl_v)
    fetch.start(("p", 3), bond.at[3], bond_v.at[1])
    fetch.start("down", down, down_v)
    fetch.start(("p", 2), bond.at[2], bond_v.at[0])
    fetch.start("up", up, up_v)
    outs = Fetch(sems)
    outs.used = fetch.used
    fetch.wait(("xh", 0), ("xl", 0), ("p", 3))
    x = (xh_v[0], xl_v[0])
    moved = split(product(x, (bond_v[1, 0], bond_v[1, 1])))
    fetch.wait("down")
    d_v[...] = product((down_v[0], down_v[1]), moved)
    outs.start("d", d_v, d_out.at[0])
    fetch.wait(("p", 2))
    moved = split(product(x, (bond_v[0, 0], bond_v[0, 1])))
    fetch.wait("up")
    u_v[...] = product((up_v[0], up_v[1]), moved)
    outs.start("u", u_v, u_out.at[0])
    outs.wait_all()


BOND_TERMS = ((0, 0), (4, 2), (1, 4))


def bond_local_kernel(high, low, bond, stack, out, *refs):
    xh_v, xl_v, bond_v, stack_v, out_v, sems = refs
    fetch = Fetch(sems)
    start_state(fetch, 0, high, low, xh_v, xl_v)
    for k, (a, matrix) in enumerate(BOND_TERMS):
        fetch.start(("p", k), bond.at[a], bond_v.at[k])
        fetch.start(("r", k), stack.at[matrix], stack_v.at[k])
    total = None
    for k in range(3):
        fetch.wait(("xh", 0), ("xl", 0), ("p", k))
        moved = split(product((xh_v[0], xl_v[0]), (bond_v[k, 0], bond_v[k, 1])))
        fetch.wait(("r", k))
        value = product((stack_v[k, 0], stack_v[k, 1]), moved)
        total = value if total is None else total + value
    out_v[...] = total
    outs = Fetch(sems)
    outs.used = fetch.used
    outs.start("out", out_v, out.at[0])
    outs.wait_all()


def rough(left, right):
    return jnp.dot(left, right, preferred_element_type=jnp.float32)


def site_send_quarter(place_ref, high, four_ref, up_ref, down_ref, d_ref, u_ref, z_ref):
    size = high.shape[0]
    for s in range(3):
        z_ref[s] = rough(high[:, s * size : (s + 1) * size], four_ref[s, 0]).astype(BF16)
    d_ref[0], d_ref[1] = cut_columns(rough(down_ref[0], join(z_ref[0], z_ref[1])), 2)
    u_ref[0], u_ref[1] = cut_columns(rough(up_ref[0], join(z_ref[1], z_ref[2])), 2)


def site_local_quarter(place_ref, high, mix_ref, stack_ref, z_ref, out_ref):
    size = high.shape[0]

    def merged(s, *matrices):
        right = join(*[mix_ref[m, 0] for m in matrices])
        return cut_columns(rough(high[:, s * size : (s + 1) * size], right), len(matrices))

    p0, p1 = merged(0, 0, 3)
    more0, more1, p2 = merged(1, 1, 2, 6)
    last2, last1 = merged(2, 5, 4)
    mixed = join(p0 + more0, p1 + more1 + last1, p2 + last2).astype(BF16)
    y = cut_columns(rough(stack_ref[0, 0], mixed), 3)
    for s in range(3):
        out_ref[s] = y[s] + rough(stack_ref[1 + s, 0], z_ref[s])


def bond_send_quarter(place_ref, high, p_ref, up_ref, down_ref, d_ref, u_ref):
    right = join(p_ref[3, 0], p_ref[2, 0])
    down, up = cut_columns(rough(high[...], right).astype(BF16), 2)
    d_ref[0] = rough(down_ref[0], down)
    u_ref[0] = rough(up_ref[0], up)


def bond_local_quarter(place_ref, high, p_ref, stack_ref, out_ref):
    right = join(*[p_ref[a, 0] for a, _ in BOND_TERMS])
    moved = cut_columns(rough(high[...], right).astype(BF16), 3)
    total = None
    for value, (_, matrix) in zip(moved, BOND_TERMS):
        value = rough(stack_ref[matrix, 0], value)
        total = value if total is None else total + value
    out_ref[0] = total


def site_first_kernel(high, low, four_ref, mix_ref, zh, zl, ph, pl_out):
    x = [columns_of(high, low, s) for s in range(3)]
    for s in range(3):
        zh[s], zl[s] = split(product(x[s], pair_of(four_ref, s)))
        total = None
        for source, matrix in TERMS[s]:
            value = product(x[source], pair_of(mix_ref, matrix))
            total = value if total is None else total + value
        ph[s], pl_out[s] = split(total)


def first_products(pair, four, mix):
    size = four.shape[-1]
    width = size // 2
    thirds = pl.BlockSpec((3, size, width), lambda i: (0, 0, i))
    state = pl.BlockSpec((size, 3 * size), lambda i: (0, 0))
    return pl.pallas_call(
        site_first_kernel,
        grid=(2,),
        in_specs=[state, state]
        + [pl.BlockSpec((m.shape[0], 2, size, width), lambda i: (0, 0, 0, i)) for m in (four, mix)],
        out_specs=[thirds] * 4,
        out_shape=[jax.ShapeDtypeStruct((3, size, size), BF16)] * 4,
        compiler_params=params(),
        cost_estimate=pl.CostEstimate(
            flops=10 * UNIT, bytes_accessed=16 * 2**20, transcendentals=0
        ),
    )(*pair, four, mix)


def site_first_send(zh, zl, up, down, d_out, u_out, zh_v, zl_v, up_v, down_v, d_v, u_v, sems):
    fetch = Fetch(sems)
    for s in (1, 0, 2):
        fetch.start(("zh", s), zh.at[s], zh_v.at[s])
        fetch.start(("zl", s), zl.at[s], zl_v.at[s])
        if s == 1:
            fetch.start("down", down, down_v)
            fetch.start("up", up, up_v)
    outs = Fetch(sems)
    outs.used = fetch.used
    for s in (1, 0, 2):
        fetch.wait(("zh", s), ("zl", s), "down", "up")
        pair = (zh_v[s], zl_v[s])
        if s < 2:
            d_v[s] = product((down_v[0], down_v[1]), pair)
            outs.start(("d", s), d_v.at[s], d_out.at[s])
        if s > 0:
            u_v[s - 1] = product((up_v[0], up_v[1]), pair)
            outs.start(("u", s), u_v.at[s - 1], u_out.at[s - 1])
    outs.wait_all()


def site_first_local(ph, pl_in, stack, zh, zl, out, ph_v, pl_v, stack_v, zh_v, zl_v, out_v, sems):
    fetch = Fetch(sems)
    for s in range(3):
        if s == 0:
            fetch.start(("stack", 0), stack.at[0], stack_v.at[0])
        fetch.start(("ph", s), ph.at[s], ph_v.at[s])
        fetch.start(("pl", s), pl_in.at[s], pl_v.at[s])
        fetch.start(("stack", 1 + s), stack.at[1 + s], stack_v.at[1 + s])
        fetch.start(("zh", s), zh.at[s], zh_v.at[s])
        fetch.start(("zl", s), zl.at[s], zl_v.at[s])
    outs = Fetch(sems)
    outs.used = fetch.used
    for s in range(3):
        fetch.wait(("stack", 0), ("ph", s), ("pl", s))
        y = product((stack_v[0, 0], stack_v[0, 1]), (ph_v[s], pl_v[s]))
        fetch.wait(("stack", 1 + s), ("zh", s), ("zl", s))
        out_v[s] = y + product((stack_v[1 + s, 0], stack_v[1 + s, 1]), (zh_v[s], zl_v[s]))
        outs.start(("out", s), out_v.at[s], out.at[s])
    outs.wait_all()


UNIT = 6 * 512**3


def quarter_call(kernel, place, operands, outs, products):
    size = operands[0][1].shape[0]
    width = size // 4

    def spec(is_whole, array):
        lead = (0,) * (array.ndim - 1)
        if is_whole:
            return pl.BlockSpec(array.shape, lambda i, p: lead + (0,))
        return pl.BlockSpec(array.shape[:-1] + (width,), lambda i, p: lead + (p[0],))

    shapes = [jax.ShapeDtypeStruct(shape + (size, width), dtype) for shape, dtype in outs]
    return pl.pallas_call(
        kernel,
        grid_spec=pltpu.PrefetchScalarGridSpec(
            num_scalar_prefetch=1,
            grid=(1,),
            in_specs=[spec(*operand) for operand in operands],
            out_specs=[spec(True, shape) for shape in shapes],
        ),
        out_shape=shapes,
        compiler_params=params(),
        cost_estimate=pl.CostEstimate(
            flops=products * UNIT // 4, bytes_accessed=12 * 2**20, transcendentals=0
        ),
    )(place, *[array for _, array in operands])


def full_call(kernel, operands, outs, scratch, copies, products):
    anywhere = pl.BlockSpec(memory_space=pl.ANY)
    return pl.pallas_call(
        kernel,
        in_specs=[anywhere] * len(operands),
        out_specs=[anywhere] * len(outs),
        out_shape=[jax.ShapeDtypeStruct(shape, dtype) for shape, dtype in outs],
        scratch_shapes=[pltpu.VMEM(shape, dtype) for shape, dtype in scratch]
        + [pltpu.SemaphoreType.DMA((copies,))],
        compiler_params=params(),
        cost_estimate=pl.CostEstimate(
            flops=products * UNIT, bytes_accessed=16 * 2**20, transcendentals=0
        ),
    )(*operands)


def state_spec(spins, step, size):
    return pl.BlockSpec((step, spins * size), lambda i: (i, 0))


def part_specs(step, parts):
    return [
        pl.BlockSpec((part.shape[0], step, part.shape[2]), lambda i: (0, i, 0)) for part in parts
    ]


def state_shapes(spins, size):
    full = (size, spins * size)
    return [jax.ShapeDtypeStruct(full, t) for t in (jnp.float32, BF16, BF16)]


def first_combine_kernel(spins, scale_ref, x_ref, *refs):
    part_refs, (y_ref, high_ref, low_ref, sums_ref) = refs[:-4], refs[-4:]
    nu = scale_ref[2:3, 0:1]
    size = part_refs[0].shape[2]
    cross = jnp.float32(0.0)
    square = jnp.float32(0.0)
    for s, total in enumerate(add_parts(spins, part_refs)):
        cut = slice(s * size, (s + 1) * size)
        y = total * nu
        y_ref[:, cut] = y
        high_ref[:, cut], low_ref[:, cut] = split(y)
        cross += jnp.sum(x_ref[:, cut] * nu * y)
        square += jnp.sum(y * y)

    @pl.when(pl.program_id(0) == 0)
    def _():
        sums_ref[...] = jnp.zeros_like(sums_ref)

    sums_ref[...] += row_of([cross, square], sums_ref.shape)


def first_combine(x, nu, parts, spins):
    size = x.shape[0]
    step = 128
    state = state_spec(spins, step, size)
    *y, sums = pl.pallas_call(
        functools.partial(first_combine_kernel, spins),
        grid=(size // step,),
        in_specs=[scalar_spec(), state] + part_specs(step, parts),
        out_specs=[state] * 3 + [scalar_spec()],
        out_shape=state_shapes(spins, size) + [SCALARS],
        compiler_params=params(),
    )(nu, x, *parts)
    return y, sums


def shift_kernel(nu_ref, parts_ref, out_ref):
    total = jnp.sum(parts_ref[...], axis=0)
    row = lax.broadcasted_iota(jnp.int32, out_ref.shape, 0)
    sigma = total[0:1, 0:1]
    tau = 1.0 / jnp.sqrt(total[0:1, 1:2])
    out_ref[...] = jnp.where(row == 0, sigma, jnp.where(row == 1, tau, nu_ref[...]))


def shift_rows(nu, parts):
    return pl.pallas_call(shift_kernel, out_shape=SCALARS, compiler_params=params())(nu, parts)


def combine_kernel(second, spins, scale_ref, w_ref, *refs):
    sigma, tau, nu = scale_ref[0:1, 0:1], scale_ref[1:2, 0:1], scale_ref[2:3, 0:1]
    if second:
        x_ref, refs = refs[0], refs[1:]
    part_refs, (out_ref, high_ref, low_ref) = refs[:-3], refs[-3:]
    size = part_refs[0].shape[2]
    for s, total in enumerate(add_parts(spins, part_refs)):
        cut = slice(s * size, (s + 1) * size)
        w = w_ref[:, cut]
        if second:
            inner = w - sigma * (nu * x_ref[:, cut])
            value = tau * tau * ((total - sigma * w) - sigma * inner)
        else:
            value = tau * (total - sigma * w)
        out_ref[:, cut] = value
        high_ref[:, cut], low_ref[:, cut] = split(value)


def combine(scales, w, x, parts, spins):
    size = w.shape[0]
    step = 128
    state = state_spec(spins, step, size)
    second = x is not None
    return pl.pallas_call(
        functools.partial(combine_kernel, second, spins),
        grid=(size // step,),
        in_specs=[scalar_spec()]
        + [state] * (2 if second else 1)
        + part_specs(step, parts),
        out_specs=[state] * 3,
        out_shape=state_shapes(spins, size),
        compiler_params=params(),
    )(scales, w, *([x] if second else []), *parts)


PAIRS = [(i, j) for j in range(5) for i in range(j + 1) if (i, j) != (4, 4)]


def gram_kernel(spins, place_ref, scale_ref, *refs):
    bases = [refs[k * spins : (k + 1) * spins] for k in range(4)]
    part_refs, out_ref = refs[4 * spins : -1], refs[-1]
    sigma, tau, nu = scale_ref[0:1, 0:1], scale_ref[1:2, 0:1], scale_ref[2:3, 0:1]
    sums = [jnp.zeros((8, 128), jnp.float32)] * len(PAIRS)
    chunk = 64
    size = part_refs[0].shape[1]
    for start in range(0, size, chunk):
        rows = slice(start, start + chunk)
        for s, total in enumerate(add_parts(spins, part_refs, rows)):
            x, y, w2, w3 = (bases[k][s][rows, :] for k in range(4))
            w = [nu * x, None, w2, w3, None]
            w[1] = tau * (y - sigma * w[0])
            w[4] = tau * (total - sigma * w[3])
            for p, (i, j) in enumerate(PAIRS):
                terms = (w[i] * w[j]).reshape(chunk // 8, 8, 128)
                sums[p] = sums[p] + jnp.sum(terms, axis=0)
    out_ref[...] = row_of([jnp.sum(value) for value in sums], out_ref.shape)


def gram_row(place, scales, states, parts, spins):
    size = states[0].shape[0]
    width = parts[0].shape[-1]
    per = size // width
    quarter = [
        pl.BlockSpec((size, width), functools.partial(lambda s, i, p: (0, s * per + p[0]), s))
        for s in range(spins)
    ]
    whole = [pl.BlockSpec(part.shape, lambda i, p: (0, 0, 0)) for part in parts]
    flat = [state for state in states for s in range(spins)]
    return pl.pallas_call(
        functools.partial(gram_kernel, spins),
        grid_spec=pltpu.PrefetchScalarGridSpec(
            num_scalar_prefetch=1,
            grid=(1,),
            in_specs=[scalar_spec()] + quarter * 4 + whole,
            out_specs=scalar_spec(),
        ),
        out_shape=SCALARS,
        compiler_params=params(),
    )(place, scales, *flat, *parts)


def weights_kernel(step_size, scale_ref, sums_ref, out_ref):
    sigma, tau, nu = scale_ref[0:1], scale_ref[1:2], scale_ref[2:3]
    total = jnp.sum(sums_ref[...], axis=0)[0:1]
    gram = {}
    for p, (i, j) in enumerate(PAIRS):
        gram[(i, j)] = jnp.broadcast_to(total[:, p : p + 1], (1, 128))
    low = {}
    inverse = []
    for j in range(4):
        pivot = gram[(j, j)]
        for k in range(j):
            pivot = pivot - low[(j, k)] * low[(j, k)]
        low[(j, j)] = jnp.sqrt(pivot)
        inverse.append(1.0 / low[(j, j)])
        for i in range(j + 1, 5):
            value = gram[(j, i)]
            for k in range(j):
                value = value - low[(i, k)] * low[(j, k)]
            low[(i, j)] = value * inverse[j]
    stretch = 1.0 / tau
    beta = [low[(j + 1, j + 1)] * inverse[j] * stretch for j in range(3)]
    alpha = []
    for j in range(4):
        value = low[(j + 1, j)] * stretch
        if j > 0:
            value = value - low[(j, j - 1)] * beta[j - 1]
        alpha.append(sigma + value * inverse[j])
    factor = step_size / 16.0
    diag = [factor * a for a in alpha]
    off = [factor * b for b in beta]
    one = jnp.ones_like(sigma)
    zero = jnp.zeros_like(sigma)
    result = {(i, j): one if i == j else zero for i in range(4) for j in range(i, 4)}

    def entry(table, i, j):
        return table[(min(i, j), max(i, j))]

    for degree in range(8, 0, -1):
        fresh = {}
        for i in range(4):
            for j in range(i, 4):
                value = diag[i] * entry(result, i, j)
                if i > 0:
                    value = value + off[i - 1] * entry(result, i - 1, j)
                if i < 3:
                    value = value + off[i] * entry(result, i + 1, j)
                value = value * (1.0 / degree)
                fresh[(i, j)] = one + value if i == j else value
        result = fresh
    for squaring in range(4):
        fresh = {}
        for i in range(4):
            for j in range(i, 4):
                if squaring == 3 and i > 0:
                    continue
                value = entry(result, i, 0) * entry(result, 0, j)
                for k in range(1, 4):
                    value = value + entry(result, i, k) * entry(result, k, j)
                fresh[(i, j)] = value
        result = fresh
    column = [result[(0, j)] for j in range(4)]
    size = jnp.sqrt(sum(c * c for c in column))
    c = [None] * 4
    for i in range(3, -1, -1):
        value = column[i]
        for j in range(i + 1, 4):
            value = value - low[(j, i)] * c[j]
        c[i] = value * inverse[i]
    norm = low[(0, 0)] / nu
    c = [norm * v for v in c]
    rows = [(c[0] - c[1] * tau * sigma) * nu, c[1] * tau, c[2], c[3], 1.0 / (norm * size)]
    for p, value in enumerate(rows):
        out_ref[p : p + 1, :] = value
    for p in range(len(rows), 8):
        out_ref[p : p + 1, :] = zero


def basis_weights(scales, sums, step_size):
    return pl.pallas_call(
        functools.partial(weights_kernel, step_size),
        out_shape=SCALARS,
        compiler_params=params(),
    )(scales, sums)


def result_kernel(place_ref, weight_ref, *refs):
    value = weight_ref[0:1, 0:1] * refs[0][...]
    for k in range(1, 4):
        value = value + weight_ref[k : k + 1, 0:1] * refs[k][...]
    refs[4][...] = value


def weighted(place, weights, states, rows):
    size, columns = states[0].shape
    step = 128 if rows is None else rows
    if rows is None:
        spec = pl.BlockSpec((step, columns), lambda i, p: (i, 0))
    else:
        spec = pl.BlockSpec((step, columns), lambda i, p: (p[0], 0))
    return pl.pallas_call(
        result_kernel,
        grid_spec=pltpu.PrefetchScalarGridSpec(
            num_scalar_prefetch=1,
            grid=(size // step if rows is None else 1,),
            in_specs=[scalar_spec()] + [spec] * 4,
            out_specs=pl.BlockSpec((step, columns), lambda i, p: (i, 0)),
        ),
        out_shape=jax.ShapeDtypeStruct((size if rows is None else rows, columns), jnp.float32),
        compiler_params=params(),
    )(place, weights, *states)


def evolve(place, x, nu, apply_op, step_size, spins):
    parts, _ = apply_op(split_state(x), None, "first")
    (y, *y_split), sums = first_combine(x, nu, parts, spins)
    parts, totals = apply_op(y_split, sums, "middle")
    scales = shift_rows(nu, totals)
    w2, *w2_split = combine(scales, y, x, parts, spins)
    parts, _ = apply_op(w2_split, None, "middle")
    w3, *w3_split = combine(scales, w2, None, parts, spins)
    parts, _ = apply_op(w3_split, None, "last")
    states = [x, y, w2, w3]
    row = gram_row(place, scales, states, parts, spins)
    weights = basis_weights(scales, exchange(row, ("col", "sec")), step_size)
    return states, weights


def body(site_tensor, left_env, right_env, bond_env, sector_sizes):
    col_rows = site_tensor.shape[0]
    size = left_env.shape[2]
    sector = lax.axis_index("sec")
    last = lax.axis_size("sec") - 1
    place = lax.axis_index("col").reshape(1).astype(jnp.int32)

    left = left_env[0]
    site_block = site_tensor[:, 0]
    site_full = gather_col(site_block, 0)
    right_blocks = gather_col(right_env, 0)
    site_nu = inverse_norm(exchange(norm_row(site_block), ("col", "sec")))

    below_four = to_next(left[4])
    above_four = to_previous(left[4])
    below_sum = to_next(left[0] + left[1] + ANISOTROPY * left[4])
    above_sum = to_previous(left[0] - left[1] + ANISOTROPY * left[4])
    flags = jnp.stack([sector < last, sector > 0]).astype(jnp.int32)
    four, mix = left_parts(flags, left, below_sum, below_four, above_sum, above_four)
    stack, up, down = right_parts(right_blocks)
    bond = bond_parts(bond_env[0])

    def send_sums(sums, after):
        if sums is None:
            return None
        sums, _ = lax.optimization_barrier((sums, after))
        return exchange(sums, "sec")

    matrix = (size, size)
    thirds = ((3,) + matrix, BF16)
    pairs = ((2,) + matrix, BF16)
    f32 = jnp.float32

    doubles = ((2,) + matrix, f32)

    def apply_site(pair, sums, stage):
        if stage == "last":
            d, u, z = quarter_call(
                site_send_quarter,
                place,
                [(True, pair[0]), (False, four), (True, up), (True, down)],
                [((2,), f32)] * 2 + [((3,), BF16)],
                7,
            )
        elif stage == "first":
            zh, zl, ph, pl_part = first_products(pair, four, mix)
            d, u = full_call(
                site_first_send,
                [zh, zl, up, down],
                [doubles] * 2,
                [thirds, thirds, pairs, pairs, doubles, doubles],
                16,
                4,
            )
        else:
            d, u, zh, zl = full_call(
                site_send_kernel,
                [pair[0], pair[1], four, up, down],
                [doubles] * 2 + [thirds] * 2,
                [thirds, thirds, ((3, 2) + matrix, BF16), pairs, pairs, thirds, thirds]
                + [doubles] * 2,
                24,
                7,
            )
        totals = send_sums(sums, u)
        d, u = to_previous(d), to_next(u)
        if stage == "last":
            (local,) = quarter_call(
                site_local_quarter,
                place,
                [(True, pair[0]), (False, mix), (True, stack), (True, z)],
                [((3,), f32)],
                13,
            )
        elif stage == "first":
            (local,) = full_call(
                site_first_local,
                [ph, pl_part, stack, zh, zl],
                [((3,) + matrix, f32)],
                [thirds, thirds, ((4, 2) + matrix, BF16), thirds, thirds, ((3,) + matrix, f32)],
                24,
                6,
            )
        else:
            (local,) = full_call(
                site_local_kernel,
                [pair[0], pair[1], mix, stack, zh, zl],
                [((3,) + matrix, f32)],
                [thirds, thirds, ((7, 2) + matrix, BF16), ((4, 2) + matrix, BF16), thirds, thirds]
                + [((3,) + matrix, f32)],
                32,
                13,
            )
        return [local, d, u], totals

    states, weights = evolve(place, site_full, site_nu, apply_site, -TIME_STEP, 3)
    evolved = weighted(place, weights, states, None)
    out_site = weighted(place, weights, states, col_rows)[:, None, :]
    gram = lax.dot_general(evolved, evolved, (((1,), (1,)), ((), ())), precision=HIGHEST)
    live = (jnp.arange(size) < sector_sizes[0]).astype(jnp.float32)
    gram = gram + (1.0 - live)[:, None] * jnp.eye(size, dtype=jnp.float32)
    factor = jnp.linalg.cholesky(gram[None])[0]
    bond_scale = math.sqrt(3.0 * size)
    start = factor * live[:, None] * live[None, :] / bond_scale
    bond_nu = jnp.broadcast_to(weights[4:5] * bond_scale, (8, 128))

    single = ((1,) + matrix, BF16)

    def apply_bond(pair, sums, stage):
        if stage == "last":
            down_term, up_term = quarter_call(
                bond_send_quarter,
                place,
                [(True, pair[0]), (False, bond), (True, up), (True, down)],
                [((1,), f32)] * 2,
                4,
            )
        else:
            down_term, up_term = full_call(
                bond_send_kernel,
                [pair[0], pair[1], bond, up, down],
                [((1,) + matrix, f32)] * 2,
                [single, single, ((2, 2) + matrix, BF16), pairs, pairs] + [(matrix, f32)] * 2,
                8,
                4,
            )
        totals = send_sums(sums, up_term)
        down_term, up_term = to_previous(down_term), to_next(up_term)
        if stage == "last":
            (local,) = quarter_call(
                bond_local_quarter,
                place,
                [(True, pair[0]), (False, bond), (True, stack)],
                [((1,), f32)],
                6,
            )
        else:
            (local,) = full_call(
                bond_local_kernel,
                [pair[0], pair[1], bond, stack],
                [((1,) + matrix, f32)],
                [single, single, ((3, 2) + matrix, BF16), ((3, 2) + matrix, BF16), (matrix, f32)],
                9,
                6,
            )
        return [local, down_term, up_term], totals

    states, weights = evolve(place, start, bond_nu, apply_bond, TIME_STEP, 1)
    out_bond = weighted(place, weights, states, col_rows)[:, None, :]
    return (out_site, out_bond)


def solution(mesh):
    in_specs = (
        P("col", "sec", None),
        P("sec", None, None, None),
        P("sec", None, None, "col"),
        P("sec", None, None, None),
        P("sec"),
    )
    out_specs = (P("col", "sec", None), P("col", "sec", None))
    return jax.shard_map(body, mesh=mesh, in_specs=in_specs, out_specs=out_specs, check_vma=False)
```

```python
import functools
import math

import jax
import jax.numpy as jnp
from jax import lax
from jax.experimental import pallas as pl
from jax.experimental.pallas import tpu as pltpu
from jax.sharding import PartitionSpec as P

KRYLOV = 4
HIGHEST = lax.Precision.HIGHEST
ROOT_TWO = math.sqrt(2.0)
ANISOTROPY = 0.5
TIME_STEP = 0.1
VMEM_LIMIT = 56 * 1024 * 1024


def to_next(block):
    count = lax.axis_size("sec")
    return lax.ppermute(block, "sec", [(i, i + 1) for i in range(count - 1)])


def to_previous(block):
    count = lax.axis_size("sec")
    return lax.ppermute(block, "sec", [(i + 1, i) for i in range(count - 1)])


def gather_col(block, axis):
    return lax.all_gather(block, "col", axis=axis, tiled=True)


def params():
    return pltpu.CompilerParams(vmem_limit_bytes=VMEM_LIMIT)


def exchange(rows, axis):
    count = lax.axis_size(axis) if isinstance(axis, str) else lax.axis_size(axis[0]) * lax.axis_size(axis[1])
    sent = jnp.broadcast_to(rows[None], (count,) + rows.shape)
    return lax.all_to_all(sent, axis, 0, 0)


def row_of(values, shape):
    lane = lax.broadcasted_iota(jnp.int32, shape, 1)
    row = lax.broadcasted_iota(jnp.int32, shape, 0)
    out = jnp.zeros(shape, jnp.float32)
    for p, value in enumerate(values):
        out = jnp.where((lane == p) & (row == 0), value, out)
    return out


def add_parts(spins, part_refs, rows=slice(None)):
    local = part_refs[0]
    if spins == 1:
        return [local[0, rows, :] + part_refs[1][0, rows, :] + part_refs[2][0, rows, :]]
    down0, down1 = (part_refs[1][k, rows, :] for k in range(2))
    up1, up2 = (part_refs[2][k, rows, :] for k in range(2))
    return [local[0, rows, :] + up1, local[1, rows, :] + (up2 + down0), local[2, rows, :] + down1]


BF16 = jnp.bfloat16


def split(value):
    high = value.astype(BF16)
    return high, (value - high.astype(jnp.float32)).astype(BF16)


def product(left, right):
    def dot(a, b):
        return jnp.dot(a, b, preferred_element_type=jnp.float32)

    return dot(left[0], right[0]) + (dot(left[0], right[1]) + dot(left[1], right[0]))


SCALARS = jax.ShapeDtypeStruct((8, 128), jnp.float32)


def scalar_spec():
    return pl.BlockSpec((8, 128), lambda *i: (0, 0))


def norm_kernel(a_ref, out_ref):
    a = a_ref[...]
    out_ref[...] = row_of([jnp.sum(a * a)], out_ref.shape)


def norm_row(block):
    return pl.pallas_call(norm_kernel, out_shape=SCALARS, compiler_params=params())(block)


def inverse_norm_kernel(parts_ref, out_ref):
    total = jnp.sum(parts_ref[...], axis=0)
    out_ref[...] = jnp.broadcast_to(1.0 / jnp.sqrt(total[0:1, 0:1]), out_ref.shape)


def inverse_norm(parts):
    return pl.pallas_call(inverse_norm_kernel, out_shape=SCALARS, compiler_params=params())(parts)


def split_kernel(x_ref, high_ref, low_ref):
    high_ref[...], low_ref[...] = split(x_ref[...])


def split_state(x):
    rows, columns = x.shape
    step = 128
    spec = pl.BlockSpec((step, columns), lambda i: (i, 0))
    return pl.pallas_call(
        split_kernel,
        grid=(rows // step,),
        in_specs=[spec],
        out_specs=[spec] * 2,
        out_shape=[jax.ShapeDtypeStruct((rows, columns), BF16)] * 2,
        compiler_params=params(),
    )(x)


def turned_kernel(place_ref, own_ref, one_ref, two_ref, three_ref, up_ref, down_ref):
    half = ROOT_TWO / 2
    for step, ref in enumerate((own_ref, one_ref, two_ref, three_ref)):
        owner = lax.rem(place_ref[0] + step, 4)
        width = ref.shape[1]
        size = up_ref.shape[2]
        rows = pl.ds(pl.multiple_of(owner * width, width), width)
        up_ref[0, rows, :], up_ref[1, rows, :] = split(half * ref[0:size, :].T)
        down_ref[0, rows, :], down_ref[1, rows, :] = split(half * ref[size : 2 * size, :].T)


def turned_parts(place, own, received):
    size = 4 * own.shape[1]
    vmem = pl.BlockSpec(memory_space=pltpu.VMEM)
    pair = jax.ShapeDtypeStruct((2, size, size), BF16)
    return pl.pallas_call(
        turned_kernel,
        in_specs=[pl.BlockSpec(memory_space=pltpu.SMEM)] + [vmem] * 4,
        out_specs=[vmem] * 2,
        out_shape=[pair] * 2,
        compiler_params=params(),
    )(place, own, *received)


PASSED = (1, 1, 2)


def symmetric_kernel(place_ref, own_ref, one_ref, two_ref, three_ref, stack_ref):
    width = own_ref.shape[2]

    def at(index):
        return pl.ds(pl.multiple_of(lax.rem(index, 4) * width, width), width)

    def store(row, column, r0, r1, r4):
        for k, value in enumerate((r0, r4 + r1, r4, r4 - r1, r1)):
            high, low = split(value)
            stack_ref[k, 0, at(row), at(column)] = high
            stack_ref[k, 1, at(row), at(column)] = low

    me = place_ref[0]
    for step in range(4):
        blocks = [own_ref[b, at(me + step), :] for b in range(3)]
        store(me + step, me, *blocks)
        if step > 0:
            store(me, me + step, *[block.T for block in blocks])
    for step, ref in ((1, one_ref), (2, two_ref), (3, three_ref)):
        owner = me + step
        other = owner + PASSED[step - 1]
        first = 8 * width
        parts = [ref[first + k * width : first + (k + 1) * width, :] for k in range(6)]
        store(owner, owner, *parts[0::2])
        blocks = parts[1::2]
        store(other, owner, *blocks)
        store(owner, other, *[block.T for block in blocks])


def symmetric_parts(place, own, received):
    size = own.shape[1]
    vmem = pl.BlockSpec(memory_space=pltpu.VMEM)
    return pl.pallas_call(
        symmetric_kernel,
        in_specs=[pl.BlockSpec(memory_space=pltpu.SMEM)] + [vmem] * 4,
        out_specs=vmem,
        out_shape=jax.ShapeDtypeStruct((5, 2, size, size), BF16),
        compiler_params=params(),
    )(place, own, *received)


def gather_right(place, right):
    width = right.shape[2]
    me = place[0]
    turned = right[2:4]
    symmetric = jnp.stack([right[0], right[1], right[4]])

    def rows(step):
        start = ((me + step) % 4) * width
        return lax.dynamic_slice_in_dim(symmetric, start, width, 1)

    def back(block, step):
        return lax.ppermute(block, "col", [(d, (d - step) % 4) for d in range(4)])

    flat = turned.reshape(-1, width)
    messages = [
        jnp.concatenate([flat, jnp.stack([rows(0), rows(passed)], axis=1).reshape(-1, width)])
        for passed in PASSED
    ]
    got = {step: back(messages[step - 1], step) for step in (1, 3, 2)}
    received = [got[step] for step in (1, 2, 3)]
    return flat, symmetric, received


def left_kernel(flag_ref, left_ref, bsum_ref, bfour_ref, asum_ref, afour_ref, four_ref, mix_ref):
    has_above, has_below = flag_ref[0], flag_ref[1]
    for k, value in enumerate((bfour_ref[...], left_ref[4], afour_ref[...])):
        four_ref[k, 0], four_ref[k, 1] = split(value)
    raise_here = jnp.where(has_above > 0, ROOT_TWO * left_ref[2], 0.0)
    lower_here = jnp.where(has_below > 0, ROOT_TWO * left_ref[3], 0.0)
    mixes = (
        bsum_ref[...], lower_here, left_ref[0], lower_here.T, raise_here.T, asum_ref[...], raise_here
    )
    for k, value in enumerate(mixes):
        mix_ref[k, 0], mix_ref[k, 1] = split(value)


def left_parts(flags, left, below_sum, below_four, above_sum, above_four):
    size = left.shape[1]
    vmem = pl.BlockSpec(memory_space=pltpu.VMEM)
    return pl.pallas_call(
        left_kernel,
        in_specs=[pl.BlockSpec(memory_space=pltpu.SMEM)] + [vmem] * 5,
        out_specs=[vmem] * 2,
        out_shape=[
            jax.ShapeDtypeStruct((3, 2, size, size), BF16),
            jax.ShapeDtypeStruct((7, 2, size, size), BF16),
        ],
        compiler_params=params(),
    )(flags, left, below_sum, below_four, above_sum, above_four)


def bond_kernel(p_ref, out_ref):
    a = pl.program_id(0)
    scale = jnp.where((a == 2) | (a == 3), ROOT_TWO, 1.0).astype(jnp.float32)
    out_ref[0, 0], out_ref[0, 1] = split(scale * p_ref[0])


def bond_parts(bond):
    count, size, _ = bond.shape
    return pl.pallas_call(
        bond_kernel,
        grid=(count,),
        in_specs=[pl.BlockSpec((1, size, size), lambda i: (i, 0, 0))],
        out_specs=pl.BlockSpec((1, 2, size, size), lambda i: (i, 0, 0, 0)),
        out_shape=jax.ShapeDtypeStruct((count, 2, size, size), BF16),
        compiler_params=params(),
    )(bond)


def pair_of(ref, index):
    return ref[index, 0], ref[index, 1]


def columns_of(high_ref, low_ref, s):
    size = high_ref.shape[0]
    cut = slice(s * size, (s + 1) * size)
    return high_ref[:, cut], low_ref[:, cut]


def join(*blocks):
    return jnp.concatenate(blocks, axis=1)


def cut_columns(value, count):
    width = value.shape[1] // count
    return [value[:, i * width : (i + 1) * width] for i in range(count)]


class Fetch:
    def __init__(self, sems):
        self.sems = sems
        self.used = 0
        self.waiting = {}

    def start(self, name, source, target):
        copy = pltpu.make_async_copy(source, target, self.sems.at[self.used])
        self.used += 1
        copy.start()
        self.waiting[name] = copy

    def wait(self, *names):
        for name in names:
            if name in self.waiting:
                self.waiting.pop(name).wait()

    def wait_all(self):
        self.wait(*list(self.waiting))


def start_state(fetch, s, high, low, high_v, low_v):
    size = high_v.shape[1]
    cut = pl.ds(s * size, size)
    fetch.start(("xh", s), high.at[:, cut], high_v.at[s])
    fetch.start(("xl", s), low.at[:, cut], low_v.at[s])


def site_send_kernel(high, low, four, up, down, *refs):
    d_out, u_out, zh, zl = refs[:4]
    xh_v, xl_v, four_v, up_v, down_v, zh_v, zl_v, d_v, u_v, sems = refs[4:]
    fetch = Fetch(sems)
    for s in (1, 0, 2):
        start_state(fetch, s, high, low, xh_v, xl_v)
        fetch.start(("four", s), four.at[s], four_v.at[s])
        if s == 1:
            fetch.start("down", down, down_v)
            fetch.start("up", up, up_v)
    outs = Fetch(sems)
    outs.used = fetch.used
    for s in (1, 0, 2):
        fetch.wait(("xh", s), ("xl", s), ("four", s))
        z = product((xh_v[s], xl_v[s]), (four_v[s, 0], four_v[s, 1]))
        zh_v[s], zl_v[s] = split(z)
        outs.start(("zh", s), zh_v.at[s], zh.at[s])
        outs.start(("zl", s), zl_v.at[s], zl.at[s])
        pair = (zh_v[s], zl_v[s])
        if s < 2:
            fetch.wait("down")
            d_v[s] = product((down_v[0], down_v[1]), pair)
            outs.start(("d", s), d_v.at[s], d_out.at[s])
        if s > 0:
            fetch.wait("up")
            u_v[s - 1] = product((up_v[0], up_v[1]), pair)
            outs.start(("u", s), u_v.at[s - 1], u_out.at[s - 1])
    outs.wait_all()


TERMS = (((0, 0), (1, 1)), ((1, 2), (0, 3), (2, 4)), ((2, 5), (1, 6)))


def site_local_kernel(high, low, mix, stack, zh, zl, out, *refs):
    xh_v, xl_v, mix_v, stack_v, zh_v, zl_v, out_v, sems = refs
    fetch = Fetch(sems)
    seen = set()
    for s in range(3):
        for source, matrix in TERMS[s]:
            if source not in seen:
                seen.add(source)
                start_state(fetch, source, high, low, xh_v, xl_v)
            fetch.start(("mix", matrix), mix.at[matrix], mix_v.at[matrix])
        if s == 0:
            fetch.start(("stack", 0), stack.at[0], stack_v.at[0])
        fetch.start(("stack", 1 + s), stack.at[1 + s], stack_v.at[1 + s])
        fetch.start(("zh", s), zh.at[s], zh_v.at[s])
        fetch.start(("zl", s), zl.at[s], zl_v.at[s])
    outs = Fetch(sems)
    outs.used = fetch.used
    for s in range(3):
        total = None
        for source, matrix in TERMS[s]:
            fetch.wait(("xh", source), ("xl", source), ("mix", matrix))
            value = product((xh_v[source], xl_v[source]), (mix_v[matrix, 0], mix_v[matrix, 1]))
            total = value if total is None else total + value
        fetch.wait(("stack", 0), ("stack", 1 + s), ("zh", s), ("zl", s))
        y = product((stack_v[0, 0], stack_v[0, 1]), split(total))
        out_v[s] = y + product((stack_v[1 + s, 0], stack_v[1 + s, 1]), (zh_v[s], zl_v[s]))
        outs.start(("out", s), out_v.at[s], out.at[s])
    outs.wait_all()


def bond_send_kernel(high, low, bond, up, down, d_out, u_out, *refs):
    xh_v, xl_v, bond_v, up_v, down_v, d_v, u_v, sems = refs
    fetch = Fetch(sems)
    start_state(fetch, 0, high, low, xh_v, xl_v)
    fetch.start(("p", 3), bond.at[3], bond_v.at[1])
    fetch.start("down", down, down_v)
    fetch.start(("p", 2), bond.at[2], bond_v.at[0])
    fetch.start("up", up, up_v)
    outs = Fetch(sems)
    outs.used = fetch.used
    fetch.wait(("xh", 0), ("xl", 0), ("p", 3))
    x = (xh_v[0], xl_v[0])
    moved = split(product(x, (bond_v[1, 0], bond_v[1, 1])))
    fetch.wait("down")
    d_v[...] = product((down_v[0], down_v[1]), moved)
    outs.start("d", d_v, d_out.at[0])
    fetch.wait(("p", 2))
    moved = split(product(x, (bond_v[0, 0], bond_v[0, 1])))
    fetch.wait("up")
    u_v[...] = product((up_v[0], up_v[1]), moved)
    outs.start("u", u_v, u_out.at[0])
    outs.wait_all()


BOND_TERMS = ((0, 0), (4, 2), (1, 4))


def bond_local_kernel(high, low, bond, stack, out, *refs):
    xh_v, xl_v, bond_v, stack_v, out_v, sems = refs
    fetch = Fetch(sems)
    start_state(fetch, 0, high, low, xh_v, xl_v)
    for k, (a, matrix) in enumerate(BOND_TERMS):
        fetch.start(("p", k), bond.at[a], bond_v.at[k])
        fetch.start(("r", k), stack.at[matrix], stack_v.at[k])
    total = None
    for k in range(3):
        fetch.wait(("xh", 0), ("xl", 0), ("p", k))
        moved = split(product((xh_v[0], xl_v[0]), (bond_v[k, 0], bond_v[k, 1])))
        fetch.wait(("r", k))
        value = product((stack_v[k, 0], stack_v[k, 1]), moved)
        total = value if total is None else total + value
    out_v[...] = total
    outs = Fetch(sems)
    outs.used = fetch.used
    outs.start("out", out_v, out.at[0])
    outs.wait_all()


def rough(left, right):
    return jnp.dot(left, right, preferred_element_type=jnp.float32)


def site_send_quarter(place_ref, high, four_ref, up_ref, down_ref, d_ref, u_ref, z_ref):
    size = high.shape[0]
    for s in range(3):
        z_ref[s] = rough(high[:, s * size : (s + 1) * size], four_ref[s, 0]).astype(BF16)
    d_ref[0], d_ref[1] = cut_columns(rough(down_ref[0], join(z_ref[0], z_ref[1])), 2)
    u_ref[0], u_ref[1] = cut_columns(rough(up_ref[0], join(z_ref[1], z_ref[2])), 2)


def site_local_quarter(place_ref, high, mix_ref, stack_ref, z_ref, out_ref):
    size = high.shape[0]

    def merged(s, *matrices):
        right = join(*[mix_ref[m, 0] for m in matrices])
        return cut_columns(rough(high[:, s * size : (s + 1) * size], right), len(matrices))

    p0, p1 = merged(0, 0, 3)
    more0, more1, p2 = merged(1, 1, 2, 6)
    last2, last1 = merged(2, 5, 4)
    mixed = join(p0 + more0, p1 + more1 + last1, p2 + last2).astype(BF16)
    y = cut_columns(rough(stack_ref[0, 0], mixed), 3)
    for s in range(3):
        out_ref[s] = y[s] + rough(stack_ref[1 + s, 0], z_ref[s])


def bond_send_quarter(place_ref, high, p_ref, up_ref, down_ref, d_ref, u_ref):
    right = join(p_ref[3, 0], p_ref[2, 0])
    down, up = cut_columns(rough(high[...], right).astype(BF16), 2)
    d_ref[0] = rough(down_ref[0], down)
    u_ref[0] = rough(up_ref[0], up)


def bond_local_quarter(place_ref, high, p_ref, stack_ref, out_ref):
    right = join(*[p_ref[a, 0] for a, _ in BOND_TERMS])
    moved = cut_columns(rough(high[...], right).astype(BF16), 3)
    total = None
    for value, (_, matrix) in zip(moved, BOND_TERMS):
        value = rough(stack_ref[matrix, 0], value)
        total = value if total is None else total + value
    out_ref[0] = total


def site_first_kernel(high, low, four_ref, mix_ref, zh, zl, ph, pl_out):
    x = [columns_of(high, low, s) for s in range(3)]
    for s in range(3):
        zh[s], zl[s] = split(product(x[s], pair_of(four_ref, s)))
        total = None
        for source, matrix in TERMS[s]:
            value = product(x[source], pair_of(mix_ref, matrix))
            total = value if total is None else total + value
        ph[s], pl_out[s] = split(total)


def first_products(pair, four, mix):
    size = four.shape[-1]
    width = size // 2
    thirds = pl.BlockSpec((3, size, width), lambda i: (0, 0, i))
    state = pl.BlockSpec((size, 3 * size), lambda i: (0, 0))
    return pl.pallas_call(
        site_first_kernel,
        grid=(2,),
        in_specs=[state, state]
        + [pl.BlockSpec((m.shape[0], 2, size, width), lambda i: (0, 0, 0, i)) for m in (four, mix)],
        out_specs=[thirds] * 4,
        out_shape=[jax.ShapeDtypeStruct((3, size, size), BF16)] * 4,
        compiler_params=params(),
        cost_estimate=pl.CostEstimate(
            flops=10 * UNIT, bytes_accessed=16 * 2**20, transcendentals=0
        ),
    )(*pair, four, mix)


def site_first_send(zh, zl, up, down, d_out, u_out, zh_v, zl_v, up_v, down_v, d_v, u_v, sems):
    fetch = Fetch(sems)
    for s in (1, 0, 2):
        fetch.start(("zh", s), zh.at[s], zh_v.at[s])
        fetch.start(("zl", s), zl.at[s], zl_v.at[s])
        if s == 1:
            fetch.start("down", down, down_v)
            fetch.start("up", up, up_v)
    outs = Fetch(sems)
    outs.used = fetch.used
    for s in (1, 0, 2):
        fetch.wait(("zh", s), ("zl", s), "down", "up")
        pair = (zh_v[s], zl_v[s])
        if s < 2:
            d_v[s] = product((down_v[0], down_v[1]), pair)
            outs.start(("d", s), d_v.at[s], d_out.at[s])
        if s > 0:
            u_v[s - 1] = product((up_v[0], up_v[1]), pair)
            outs.start(("u", s), u_v.at[s - 1], u_out.at[s - 1])
    outs.wait_all()


def site_first_local(ph, pl_in, stack, zh, zl, out, ph_v, pl_v, stack_v, zh_v, zl_v, out_v, sems):
    fetch = Fetch(sems)
    for s in range(3):
        if s == 0:
            fetch.start(("stack", 0), stack.at[0], stack_v.at[0])
        fetch.start(("ph", s), ph.at[s], ph_v.at[s])
        fetch.start(("pl", s), pl_in.at[s], pl_v.at[s])
        fetch.start(("stack", 1 + s), stack.at[1 + s], stack_v.at[1 + s])
        fetch.start(("zh", s), zh.at[s], zh_v.at[s])
        fetch.start(("zl", s), zl.at[s], zl_v.at[s])
    outs = Fetch(sems)
    outs.used = fetch.used
    for s in range(3):
        fetch.wait(("stack", 0), ("ph", s), ("pl", s))
        y = product((stack_v[0, 0], stack_v[0, 1]), (ph_v[s], pl_v[s]))
        fetch.wait(("stack", 1 + s), ("zh", s), ("zl", s))
        out_v[s] = y + product((stack_v[1 + s, 0], stack_v[1 + s, 1]), (zh_v[s], zl_v[s]))
        outs.start(("out", s), out_v.at[s], out.at[s])
    outs.wait_all()


UNIT = 6 * 512**3


def quarter_call(kernel, place, operands, outs, products):
    size = operands[0][1].shape[0]
    width = size // 4

    def spec(is_whole, array):
        lead = (0,) * (array.ndim - 1)
        if is_whole:
            return pl.BlockSpec(array.shape, lambda i, p: lead + (0,))
        return pl.BlockSpec(array.shape[:-1] + (width,), lambda i, p: lead + (p[0],))

    shapes = [jax.ShapeDtypeStruct(shape + (size, width), dtype) for shape, dtype in outs]
    return pl.pallas_call(
        kernel,
        grid_spec=pltpu.PrefetchScalarGridSpec(
            num_scalar_prefetch=1,
            grid=(1,),
            in_specs=[spec(*operand) for operand in operands],
            out_specs=[spec(True, shape) for shape in shapes],
        ),
        out_shape=shapes,
        compiler_params=params(),
        cost_estimate=pl.CostEstimate(
            flops=products * UNIT // 4, bytes_accessed=12 * 2**20, transcendentals=0
        ),
    )(place, *[array for _, array in operands])


def full_call(kernel, operands, outs, scratch, copies, products):
    anywhere = pl.BlockSpec(memory_space=pl.ANY)
    return pl.pallas_call(
        kernel,
        in_specs=[anywhere] * len(operands),
        out_specs=[anywhere] * len(outs),
        out_shape=[jax.ShapeDtypeStruct(shape, dtype) for shape, dtype in outs],
        scratch_shapes=[pltpu.VMEM(shape, dtype) for shape, dtype in scratch]
        + [pltpu.SemaphoreType.DMA((copies,))],
        compiler_params=params(),
        cost_estimate=pl.CostEstimate(
            flops=products * UNIT, bytes_accessed=16 * 2**20, transcendentals=0
        ),
    )(*operands)


def state_spec(spins, step, size):
    return pl.BlockSpec((step, spins * size), lambda i: (i, 0))


def part_specs(step, parts):
    return [
        pl.BlockSpec((part.shape[0], step, part.shape[2]), lambda i: (0, i, 0)) for part in parts
    ]


def state_shapes(spins, size):
    full = (size, spins * size)
    return [jax.ShapeDtypeStruct(full, t) for t in (jnp.float32, BF16, BF16)]


def first_combine_kernel(spins, scale_ref, x_ref, *refs):
    part_refs, (y_ref, high_ref, low_ref, sums_ref) = refs[:-4], refs[-4:]
    nu = scale_ref[2:3, 0:1]
    size = part_refs[0].shape[2]
    cross = jnp.float32(0.0)
    square = jnp.float32(0.0)
    for s, total in enumerate(add_parts(spins, part_refs)):
        cut = slice(s * size, (s + 1) * size)
        y = total * nu
        y_ref[:, cut] = y
        high_ref[:, cut], low_ref[:, cut] = split(y)
        cross += jnp.sum(x_ref[:, cut] * nu * y)
        square += jnp.sum(y * y)

    @pl.when(pl.program_id(0) == 0)
    def _():
        sums_ref[...] = jnp.zeros_like(sums_ref)

    sums_ref[...] += row_of([cross, square], sums_ref.shape)


def first_combine(x, nu, parts, spins):
    size = x.shape[0]
    step = 128
    state = state_spec(spins, step, size)
    *y, sums = pl.pallas_call(
        functools.partial(first_combine_kernel, spins),
        grid=(size // step,),
        in_specs=[scalar_spec(), state] + part_specs(step, parts),
        out_specs=[state] * 3 + [scalar_spec()],
        out_shape=state_shapes(spins, size) + [SCALARS],
        compiler_params=params(),
    )(nu, x, *parts)
    return y, sums


def shift_kernel(nu_ref, parts_ref, out_ref):
    total = jnp.sum(parts_ref[...], axis=0)
    row = lax.broadcasted_iota(jnp.int32, out_ref.shape, 0)
    sigma = total[0:1, 0:1]
    tau = 1.0 / jnp.sqrt(total[0:1, 1:2])
    out_ref[...] = jnp.where(row == 0, sigma, jnp.where(row == 1, tau, nu_ref[...]))


def shift_rows(nu, parts):
    return pl.pallas_call(shift_kernel, out_shape=SCALARS, compiler_params=params())(nu, parts)


def combine_kernel(second, spins, scale_ref, w_ref, *refs):
    sigma, tau, nu = scale_ref[0:1, 0:1], scale_ref[1:2, 0:1], scale_ref[2:3, 0:1]
    if second:
        x_ref, refs = refs[0], refs[1:]
    part_refs, (out_ref, high_ref, low_ref) = refs[:-3], refs[-3:]
    size = part_refs[0].shape[2]
    for s, total in enumerate(add_parts(spins, part_refs)):
        cut = slice(s * size, (s + 1) * size)
        w = w_ref[:, cut]
        if second:
            inner = w - sigma * (nu * x_ref[:, cut])
            value = tau * tau * ((total - sigma * w) - sigma * inner)
        else:
            value = tau * (total - sigma * w)
        out_ref[:, cut] = value
        high_ref[:, cut], low_ref[:, cut] = split(value)


def combine(scales, w, x, parts, spins):
    size = w.shape[0]
    step = 128
    state = state_spec(spins, step, size)
    second = x is not None
    return pl.pallas_call(
        functools.partial(combine_kernel, second, spins),
        grid=(size // step,),
        in_specs=[scalar_spec()]
        + [state] * (2 if second else 1)
        + part_specs(step, parts),
        out_specs=[state] * 3,
        out_shape=state_shapes(spins, size),
        compiler_params=params(),
    )(scales, w, *([x] if second else []), *parts)


PAIRS = [(i, j) for j in range(5) for i in range(j + 1) if (i, j) != (4, 4)]


def gram_kernel(spins, place_ref, scale_ref, *refs):
    bases = [refs[k * spins : (k + 1) * spins] for k in range(4)]
    part_refs, out_ref = refs[4 * spins : -1], refs[-1]
    sigma, tau, nu = scale_ref[0:1, 0:1], scale_ref[1:2, 0:1], scale_ref[2:3, 0:1]
    sums = [jnp.zeros((8, 128), jnp.float32)] * len(PAIRS)
    chunk = 64
    size = part_refs[0].shape[1]
    for start in range(0, size, chunk):
        rows = slice(start, start + chunk)
        for s, total in enumerate(add_parts(spins, part_refs, rows)):
            x, y, w2, w3 = (bases[k][s][rows, :] for k in range(4))
            w = [nu * x, None, w2, w3, None]
            w[1] = tau * (y - sigma * w[0])
            w[4] = tau * (total - sigma * w[3])
            for p, (i, j) in enumerate(PAIRS):
                terms = (w[i] * w[j]).reshape(chunk // 8, 8, 128)
                sums[p] = sums[p] + jnp.sum(terms, axis=0)
    out_ref[...] = row_of([jnp.sum(value) for value in sums], out_ref.shape)


def gram_row(place, scales, states, parts, spins):
    size = states[0].shape[0]
    width = parts[0].shape[-1]
    per = size // width
    quarter = [
        pl.BlockSpec((size, width), functools.partial(lambda s, i, p: (0, s * per + p[0]), s))
        for s in range(spins)
    ]
    whole = [pl.BlockSpec(part.shape, lambda i, p: (0, 0, 0)) for part in parts]
    flat = [state for state in states for s in range(spins)]
    return pl.pallas_call(
        functools.partial(gram_kernel, spins),
        grid_spec=pltpu.PrefetchScalarGridSpec(
            num_scalar_prefetch=1,
            grid=(1,),
            in_specs=[scalar_spec()] + quarter * 4 + whole,
            out_specs=scalar_spec(),
        ),
        out_shape=SCALARS,
        compiler_params=params(),
    )(place, scales, *flat, *parts)


def weights_kernel(step_size, scale_ref, sums_ref, out_ref):
    sigma, tau, nu = scale_ref[0:1], scale_ref[1:2], scale_ref[2:3]
    total = jnp.sum(sums_ref[...], axis=0)[0:1]
    gram = {}
    for p, (i, j) in enumerate(PAIRS):
        gram[(i, j)] = jnp.broadcast_to(total[:, p : p + 1], (1, 128))
    low = {}
    inverse = []
    for j in range(4):
        pivot = gram[(j, j)]
        for k in range(j):
            pivot = pivot - low[(j, k)] * low[(j, k)]
        low[(j, j)] = jnp.sqrt(pivot)
        inverse.append(1.0 / low[(j, j)])
        for i in range(j + 1, 5):
            value = gram[(j, i)]
            for k in range(j):
                value = value - low[(i, k)] * low[(j, k)]
            low[(i, j)] = value * inverse[j]
    stretch = 1.0 / tau
    beta = [low[(j + 1, j + 1)] * inverse[j] * stretch for j in range(3)]
    alpha = []
    for j in range(4):
        value = low[(j + 1, j)] * stretch
        if j > 0:
            value = value - low[(j, j - 1)] * beta[j - 1]
        alpha.append(sigma + value * inverse[j])
    factor = step_size / 16.0
    diag = [factor * a for a in alpha]
    off = [factor * b for b in beta]
    one = jnp.ones_like(sigma)
    zero = jnp.zeros_like(sigma)
    result = {(i, j): one if i == j else zero for i in range(4) for j in range(i, 4)}

    def entry(table, i, j):
        return table[(min(i, j), max(i, j))]

    for degree in range(8, 0, -1):
        fresh = {}
        for i in range(4):
            for j in range(i, 4):
                value = diag[i] * entry(result, i, j)
                if i > 0:
                    value = value + off[i - 1] * entry(result, i - 1, j)
                if i < 3:
                    value = value + off[i] * entry(result, i + 1, j)
                value = value * (1.0 / degree)
                fresh[(i, j)] = one + value if i == j else value
        result = fresh
    for squaring in range(4):
        fresh = {}
        for i in range(4):
            for j in range(i, 4):
                if squaring == 3 and i > 0:
                    continue
                value = entry(result, i, 0) * entry(result, 0, j)
                for k in range(1, 4):
                    value = value + entry(result, i, k) * entry(result, k, j)
                fresh[(i, j)] = value
        result = fresh
    column = [result[(0, j)] for j in range(4)]
    size = jnp.sqrt(sum(c * c for c in column))
    c = [None] * 4
    for i in range(3, -1, -1):
        value = column[i]
        for j in range(i + 1, 4):
            value = value - low[(j, i)] * c[j]
        c[i] = value * inverse[i]
    norm = low[(0, 0)] / nu
    c = [norm * v for v in c]
    rows = [(c[0] - c[1] * tau * sigma) * nu, c[1] * tau, c[2], c[3], 1.0 / (norm * size)]
    for p, value in enumerate(rows):
        out_ref[p : p + 1, :] = value
    for p in range(len(rows), 8):
        out_ref[p : p + 1, :] = zero


def basis_weights(scales, sums, step_size):
    return pl.pallas_call(
        functools.partial(weights_kernel, step_size),
        out_shape=SCALARS,
        compiler_params=params(),
    )(scales, sums)


def result_kernel(place_ref, weight_ref, *refs):
    value = weight_ref[0:1, 0:1] * refs[0][...]
    for k in range(1, 4):
        value = value + weight_ref[k : k + 1, 0:1] * refs[k][...]
    refs[4][...] = value


def weighted(place, weights, states, rows):
    size, columns = states[0].shape
    step = 128 if rows is None else rows
    if rows is None:
        spec = pl.BlockSpec((step, columns), lambda i, p: (i, 0))
    else:
        spec = pl.BlockSpec((step, columns), lambda i, p: (p[0], 0))
    return pl.pallas_call(
        result_kernel,
        grid_spec=pltpu.PrefetchScalarGridSpec(
            num_scalar_prefetch=1,
            grid=(size // step if rows is None else 1,),
            in_specs=[scalar_spec()] + [spec] * 4,
            out_specs=pl.BlockSpec((step, columns), lambda i, p: (i, 0)),
        ),
        out_shape=jax.ShapeDtypeStruct((size if rows is None else rows, columns), jnp.float32),
        compiler_params=params(),
    )(place, weights, *states)


def evolve(place, x, nu, apply_op, step_size, spins):
    parts, _ = apply_op(split_state(x), None, "first")
    (y, *y_split), sums = first_combine(x, nu, parts, spins)
    parts, totals = apply_op(y_split, sums, "middle")
    scales = shift_rows(nu, totals)
    w2, *w2_split = combine(scales, y, x, parts, spins)
    parts, _ = apply_op(w2_split, None, "middle")
    w3, *w3_split = combine(scales, w2, None, parts, spins)
    parts, _ = apply_op(w3_split, None, "last")
    states = [x, y, w2, w3]
    row = gram_row(place, scales, states, parts, spins)
    weights = basis_weights(scales, exchange(row, ("col", "sec")), step_size)
    return states, weights


def body(site_tensor, left_env, right_env, bond_env, sector_sizes):
    col_rows = site_tensor.shape[0]
    size = left_env.shape[2]
    sector = lax.axis_index("sec")
    last = lax.axis_size("sec") - 1
    place = lax.axis_index("col").reshape(1).astype(jnp.int32)

    left = left_env[0]
    site_block = site_tensor[:, 0]
    site_full = gather_col(site_block, 0)
    flat, symmetric, received = gather_right(place, right_env[0])
    parts = {}
    site_nu = inverse_norm(exchange(norm_row(site_block), ("col", "sec")))

    below_four = to_next(left[4])
    above_four = to_previous(left[4])
    below_sum = to_next(left[0] + left[1] + ANISOTROPY * left[4])
    above_sum = to_previous(left[0] - left[1] + ANISOTROPY * left[4])
    flags = jnp.stack([sector < last, sector > 0]).astype(jnp.int32)
    flags, site_nu = lax.optimization_barrier((flags, site_nu))
    four, mix = left_parts(flags, left, below_sum, below_four, above_sum, above_four)
    bond = bond_parts(bond_env[0])

    def send_sums(sums, after):
        if sums is None:
            return None
        sums, _ = lax.optimization_barrier((sums, after))
        return exchange(sums, "sec")

    matrix = (size, size)
    thirds = ((3,) + matrix, BF16)
    pairs = ((2,) + matrix, BF16)
    f32 = jnp.float32

    doubles = ((2,) + matrix, f32)

    def apply_site(pair, sums, stage):
        if stage == "last":
            d, u, z = quarter_call(
                site_send_quarter,
                place,
                [(True, pair[0]), (False, four), (True, parts["up"]), (True, parts["down"])],
                [((2,), f32)] * 2 + [((3,), BF16)],
                7,
            )
        elif stage == "first":
            zh, zl, ph, pl_part = first_products(pair, four, mix)
            tied, zh = lax.optimization_barrier((place, zh))
            parts["up"], parts["down"] = turned_parts(tied, flat, received)
            parts["stack"] = symmetric_parts(tied, symmetric, received)
            d, u = full_call(
                site_first_send,
                [zh, zl, parts["up"], parts["down"]],
                [doubles] * 2,
                [thirds, thirds, pairs, pairs, doubles, doubles],
                16,
                4,
            )
        else:
            d, u, zh, zl = full_call(
                site_send_kernel,
                [pair[0], pair[1], four, parts["up"], parts["down"]],
                [doubles] * 2 + [thirds] * 2,
                [thirds, thirds, ((3, 2) + matrix, BF16), pairs, pairs, thirds, thirds]
                + [doubles] * 2,
                24,
                7,
            )
        totals = send_sums(sums, u)
        d, u = to_previous(d), to_next(u)
        if stage == "last":
            (local,) = quarter_call(
                site_local_quarter,
                place,
                [(True, pair[0]), (False, mix), (True, parts["stack"]), (True, z)],
                [((3,), f32)],
                13,
            )
        elif stage == "first":
            (local,) = full_call(
                site_first_local,
                [ph, pl_part, parts["stack"], zh, zl],
                [((3,) + matrix, f32)],
                [thirds, thirds, ((4, 2) + matrix, BF16), thirds, thirds, ((3,) + matrix, f32)],
                24,
                6,
            )
        else:
            (local,) = full_call(
                site_local_kernel,
                [pair[0], pair[1], mix, parts["stack"], zh, zl],
                [((3,) + matrix, f32)],
                [thirds, thirds, ((7, 2) + matrix, BF16), ((4, 2) + matrix, BF16), thirds, thirds]
                + [((3,) + matrix, f32)],
                32,
                13,
            )
        return [local, d, u], totals

    states, weights = evolve(place, site_full, site_nu, apply_site, -TIME_STEP, 3)
    evolved = weighted(place, weights, states, None)
    out_site = weighted(place, weights, states, col_rows)[:, None, :]
    gram = lax.dot_general(evolved, evolved, (((1,), (1,)), ((), ())), precision=HIGHEST)
    live = (jnp.arange(size) < sector_sizes[0]).astype(jnp.float32)
    gram = gram + (1.0 - live)[:, None] * jnp.eye(size, dtype=jnp.float32)
    factor = jnp.linalg.cholesky(gram[None])[0]
    bond_scale = math.sqrt(3.0 * size)
    start = factor * live[:, None] * live[None, :] / bond_scale
    bond_nu = jnp.broadcast_to(weights[4:5] * bond_scale, (8, 128))

    single = ((1,) + matrix, BF16)

    def apply_bond(pair, sums, stage):
        if stage == "last":
            down_term, up_term = quarter_call(
                bond_send_quarter,
                place,
                [(True, pair[0]), (False, bond), (True, parts["up"]), (True, parts["down"])],
                [((1,), f32)] * 2,
                4,
            )
        else:
            down_term, up_term = full_call(
                bond_send_kernel,
                [pair[0], pair[1], bond, parts["up"], parts["down"]],
                [((1,) + matrix, f32)] * 2,
                [single, single, ((2, 2) + matrix, BF16), pairs, pairs] + [(matrix, f32)] * 2,
                8,
                4,
            )
        totals = send_sums(sums, up_term)
        down_term, up_term = to_previous(down_term), to_next(up_term)
        if stage == "last":
            (local,) = quarter_call(
                bond_local_quarter,
                place,
                [(True, pair[0]), (False, bond), (True, parts["stack"])],
                [((1,), f32)],
                6,
            )
        else:
            (local,) = full_call(
                bond_local_kernel,
                [pair[0], pair[1], bond, parts["stack"]],
                [((1,) + matrix, f32)],
                [single, single, ((3, 2) + matrix, BF16), ((3, 2) + matrix, BF16), (matrix, f32)],
                9,
                6,
            )
        return [local, down_term, up_term], totals

    states, weights = evolve(place, start, bond_nu, apply_bond, TIME_STEP, 1)
    out_bond = weighted(place, weights, states, col_rows)[:, None, :]
    return (out_site, out_bond)


def solution(mesh):
    in_specs = (
        P("col", "sec", None),
        P("sec", None, None, None),
        P("sec", None, None, "col"),
        P("sec", None, None, None),
        P("sec"),
    )
    out_specs = (P("col", "sec", None), P("col", "sec", None))
    return jax.shard_map(body, mesh=mesh, in_specs=in_specs, out_specs=out_specs, check_vma=False)
```
